32 devices in a mesh: tile: 8 (over y, x, core), chan: 4 (over z).
Axes of the slice: x: 2, y: 2, z: 4, core: 2. Of those that a mesh axis runs over, the one named last changes fastest.
Arguments:
- features: bfloat16 [64, 1536, 128], P('tile', 'chan'), may hold values from -8 to 8
- dw_weight: float32 [1536, 49], P('chan'), may hold values from -2.5 to 2.5
- dw_bias: float32 [1536], P('chan'), may hold values from -3 to 3
- ln_gain: float32 [1536], replicated, may hold values from 0.5 to 1.5
- ln_bias: float32 [1536], replicated, may hold values from -2 to 2
- w_in: bfloat16 [1536, 6144], P('tile', 'chan'), may hold values from -0.15625 to 0.15625
- b_in: float32 [6144], P('chan'), may hold values from -3 to 3
- w_out: bfloat16 [6144, 1536], P('chan', 'tile'), may hold values from -0.109375 to 0.109375
- b_out: float32 [1536], P('chan'), may hold values from -3 to 3
- gamma: float32 [1536], P('chan'), may hold values from 0.5 to 2
Outputs:
- block_out: bfloat16 [64, 1536, 128], P('tile', 'chan')
The draws below stay inside these ranges and needn't reach their ends.
All inputs are finite; a program needn't handle non-finite values.
Results may differ from the reference program's by a relative error of at most 0.015.
Values may be sent and summed in bfloat16 or wider, within the bound.
No kernel may reach another device: no remote copies, remote signals or barrier semaphores. Data moves between devices by JAX's collectives and lax.ppermute only.
A program may use at most 64 MiB of HBM per device.

```python
import math
import jax
import jax.numpy as jnp
from jax import lax

CHANNELS = 1536
EXPANDED = 6144
KERNEL = 7
WIDTH_PX = 128
HEIGHT_PX = 64
N_CHAN = 4


def draw_features(key, part):
    key_base, key_scale = jax.random.split(key, 2)
    scale = jnp.exp(jax.random.uniform(key_scale, (HEIGHT_PX, 1, WIDTH_PX), jnp.float32, math.log(0.5), math.log(2.0)))
    values = jnp.clip(jax.random.normal(key_base, (HEIGHT_PX, CHANNELS, WIDTH_PX), jnp.float32), -4.0, 4.0) * scale
    return values.astype(jnp.bfloat16)


def draw_dw_weight(key, part):
    position = jnp.arange(CHANNELS, dtype=jnp.float32)[:, None] / max(CHANNELS - 1, 1)
    shape_taps = (CHANNELS, KERNEL * KERNEL)
    rising = jnp.exp(position * math.log(3.0))
    values = jnp.clip(jax.random.normal(key, shape_taps, jnp.float32), -4.0, 4.0) / 7.0 * rising
    return values.astype(jnp.float32)


def with_spikes(result, rng, source, target, parts, factor):
    owner, partner = [(jnp.arange(result.shape[axis_at]) // (result.shape[axis_at] // parts)).reshape([-1 if axis == axis_at else 1 for axis in range(result.ndim)]) for axis_at in (source, target)]
    chosen = jax.random.permutation(rng, parts)[partner]
    strong = (owner == chosen) | (owner == (partner + parts // 2) % parts)
    return jnp.where(strong, factor * result, result)


def level_of(rng, extent, cuts, smallest, high):
    loudness, own = 1.0, jax.random.fold_in(rng, 6)
    for dim, parts in cuts:
        steps = jnp.exp(jax.random.uniform(jax.random.fold_in(own, dim), (parts,), jnp.float32, smallest / len(cuts), high / len(cuts)))
        loudness = loudness * jnp.repeat(steps, extent[dim] // parts).reshape([-1 if axis == dim else 1 for axis in range(len(extent))])
    return loudness


def normal_values(own_key, extent, scale, limit, cuts=(), held_as=jnp.bfloat16):
    entries = jax.random.normal(own_key, extent, jnp.float32) * scale
    if len(cuts) > 0:
        entries = level_of(own_key, extent, cuts, -0.22, 0.18) * entries
    return jnp.clip(entries, min=-limit, max=limit).astype(held_as)


def bell_draw_with(stream_key, shape, deviation, limit, shards, heavy, kind=jnp.bfloat16):
    result = deviation * jax.random.normal(stream_key, shape, jnp.float32)
    if shards:
        result = result * level_of(stream_key, shape, shards, -0.22, 0.18)
    return jnp.clip(with_spikes(result, jax.random.fold_in(stream_key, 3), *heavy), -limit, limit).astype(kind)


def setup_inputs(seed: int = 0) -> dict:
    streams_of = jax.random.split(jax.random.key(seed), 11)
    features = draw_features(jax.random.fold_in(streams_of[10], 71), 0)
    dw_weight = draw_dw_weight(jax.random.fold_in(streams_of[10], 71), 0)
    dw_bias = normal_values(streams_of[2], (CHANNELS,), 0.5, 3.0, ((0, 4),), jnp.float32)
    ln_gain = jnp.clip(1.0 + 0.1 * jax.random.normal(streams_of[3], (CHANNELS,), jnp.float32), 0.5, 1.5)
    ln_bias = normal_values(streams_of[4], (CHANNELS,), 0.3, 2.0, (), jnp.float32)
    w_in = normal_values(streams_of[5], (CHANNELS, EXPANDED), CHANNELS ** -0.5, 0.15625, ((0, 8), (1, 4)))
    b_in = normal_values(streams_of[6], (EXPANDED,), 0.5, 3.0, ((0, 4),), jnp.float32)
    w_out = bell_draw_with(streams_of[7], (EXPANDED, CHANNELS), EXPANDED ** -0.5, 0.109375, ((0, 4), (1, 8)), (0, 1, 8, 2.0))
    b_out = normal_values(streams_of[8], (CHANNELS,), 0.5, 3.0, ((0, 4),), jnp.float32)
    gamma = jnp.clip(jnp.exp(math.log(2.0) - 1.3862944 * jax.random.uniform(streams_of[9], (CHANNELS,), jnp.float32) ** level_of(streams_of[9], (CHANNELS,), ((0, 4),), -0.2, 0.2)), 0.5, 2.0)
    return {"features": features, "dw_weight": dw_weight, "dw_bias": dw_bias, "ln_gain": ln_gain, "ln_bias": ln_bias, "w_in": w_in, "b_in": b_in, "w_out": w_out, "b_out": b_out, "gamma": gamma}


def reference(features, dw_weight, dw_bias, ln_gain, ln_bias, w_in, b_in, w_out, b_out, gamma):
    feature_float = features.astype(jnp.float32)
    padded = jnp.pad(feature_float, ((3, 3), (0, 0), (3, 3)))
    convolved = jnp.zeros_like(feature_float) + dw_bias[None, :, None]
    for tap_row in range(KERNEL):
        for tap_col in range(KERNEL):
            window = padded[tap_row:tap_row + HEIGHT_PX, :, tap_col:tap_col + WIDTH_PX]
            convolved = convolved + window * dw_weight[:, tap_row * KERNEL + tap_col][None, :, None]
    conv_out = convolved.astype(jnp.bfloat16)
    values = conv_out.astype(jnp.float32)
    average = lax.optimization_barrier(jnp.mean(values, axis=1, keepdims=True))
    centered = values - average
    variance = lax.optimization_barrier(jnp.mean(centered * centered, axis=1, keepdims=True))
    normed = (centered * lax.rsqrt(variance + 1e-06) * ln_gain[None, :, None] + ln_bias[None, :, None]).astype(jnp.bfloat16)
    flat = jnp.transpose(normed, (0, 2, 1)).reshape(HEIGHT_PX * WIDTH_PX, CHANNELS)
    group = EXPANDED // N_CHAN
    w_in_groups = jnp.transpose(w_in.reshape(CHANNELS, N_CHAN, group), (1, 0, 2))
    b_in_groups = b_in.reshape(N_CHAN, group)
    w_out_groups = w_out.reshape(N_CHAN, group, CHANNELS)

    def add_group(running, pieces):
        weight_in, bias_in, weight_out = pieces
        pre_act = jnp.dot(flat, weight_in, preferred_element_type=jnp.float32) + bias_in[None, :]
        hidden = jax.nn.gelu(pre_act, approximate=False).astype(jnp.bfloat16)
        partial_out = jnp.dot(hidden, weight_out, preferred_element_type=jnp.float32).astype(jnp.bfloat16)
        partial_out = lax.optimization_barrier(partial_out)
        return (running + partial_out.astype(jnp.float32), None)
    start_sum = jnp.zeros((HEIGHT_PX * WIDTH_PX, CHANNELS), jnp.float32)
    summed, _ = lax.scan(add_group, start_sum, (w_in_groups, b_in_groups, w_out_groups))
    projected = (summed + b_out[None, :]).reshape(HEIGHT_PX, WIDTH_PX, CHANNELS)
    projected = jnp.transpose(projected, (0, 2, 1))
    return (feature_float + gamma[None, :, None] * projected).astype(jnp.bfloat16)
```

```python
import functools

import jax
import jax.numpy as jnp
from jax import lax
from jax.experimental import pallas as pl
from jax.experimental.pallas import tpu as pltpu
from jax.sharding import PartitionSpec as P

SIDE = 7
REACH = SIDE // 2
CHUNKS = 2
VMEM_LIMIT = 48 * 1024 * 1024
EPSILON = 1e-06


def conv_kernel(plan, *refs):
    sources, taps_ref, out_ref, held = refs[:-3], refs[-3], refs[-2], refs[-1]
    rows, channels, width = held.shape
    group = 16
    column = lax.broadcasted_iota(jnp.int32, (1, group, width), 2)

    def one_group(i, carry):
        at = pl.ds(pl.multiple_of(i * group, group), group)
        image = jnp.stack([sources[s][r, at, :] for s, r in plan]).astype(jnp.float32)
        taps = taps_ref[at, :]
        bias = taps[:, SIDE * SIDE : SIDE * SIDE + 1][None]
        total = jnp.broadcast_to(bias, (rows, group, width))
        for b in range(SIDE):
            part = None
            for a in range(SIDE):
                tap = SIDE * a + b
                term = image[a : a + rows] * taps[:, tap : tap + 1][None]
                part = term if part is None else part + term
            offset = b - REACH
            if offset:
                part = pltpu.roll(part, (-offset) % width, 2)
                inside = column < width - offset if offset > 0 else column >= -offset
                part = jnp.where(inside, part, 0.0)
            total = total + part
        held[:, at, :] = total
        return carry

    lax.fori_loop(0, channels // group, one_group, 0)
    for row in range(rows):
        out_ref[row] = held[row].T.astype(out_ref.dtype)


def conv_chunk(first, rows, low, features, high, taps):
    height, slab, width = features.shape
    names, plan = ["features"], []
    for row in range(first - REACH, first + rows + REACH):
        if row < 0:
            name, index = "low", row + REACH
        elif row < height:
            name, index = "features", row
        else:
            name, index = "high", row - height
        if name not in names:
            names.append(name)
        plan.append((names.index(name), index))
    arrays = [{"features": features, "low": low, "high": high}[name] for name in names]
    block = 128
    return pl.pallas_call(
        functools.partial(conv_kernel, tuple(plan)),
        grid=(slab // block,),
        in_specs=[pl.BlockSpec((a.shape[0], block, width), lambda i: (0, i, 0)) for a in arrays]
        + [pl.BlockSpec((block, taps.shape[1]), lambda i: (i, 0))],
        out_specs=pl.BlockSpec((rows, width, block), lambda i: (0, 0, i)),
        out_shape=jax.ShapeDtypeStruct((rows, width, slab), jnp.bfloat16),
        scratch_shapes=[pltpu.VMEM((rows, block, width), jnp.float32)],
        compiler_params=pltpu.CompilerParams(vmem_limit_bytes=VMEM_LIMIT),
        cost_estimate=pl.CostEstimate(
            flops=2 * SIDE * SIDE * rows * slab * width,
            bytes_accessed=4 * rows * slab * width,
            transcendentals=0,
        ),
        name="depthwise",
    )(*arrays, taps)


def line_places(z):
    low_half = z < 2
    return z ^ 1, jnp.where(low_half, 2, 1), jnp.where(low_half, 3, 0)


def mlp_kernel(*refs):
    own, near, mid_inner, mid_outer, far_inner, far_outer = refs[:6]
    w_in_parts, w_out_parts = refs[6:14], refs[14:22]
    gain_ref, shift_ref, b_in_ref = refs[22:25]
    out_refs = refs[25:29]
    x, w_in, w_out, hidden, x_sem, in_sem, out_sem = refs[29:]
    pixels, channels = x.shape
    slab = own.shape[1]
    units = hidden.shape[1]
    shard = w_in_parts[0].shape[0]
    z, t = lax.axis_index("chan"), lax.axis_index("tile")
    pair, mid, far = line_places(z)
    inner = jnp.logical_or(z == 1, z == 2)

    def slab_copy(part, place, sem):
        at = pl.ds(pl.multiple_of(place * slab, 128), slab)
        return pltpu.make_async_copy(part, x.at[:, at], x_sem.at[sem])

    slab_copy(own, z, 0).start()
    slab_copy(near, pair, 1).start()

    @pl.when(inner)
    def _():
        slab_copy(mid_inner, mid, 2).start()
        slab_copy(far_inner, far, 3).start()

    @pl.when(jnp.logical_not(inner))
    def _():
        slab_copy(mid_outer, mid, 2).start()
        slab_copy(far_outer, far, 3).start()

    def shard_copy(part, target, k, sems):
        at = pl.ds(pl.multiple_of((t ^ k) * shard, 16), shard)
        return pltpu.make_async_copy(part, target.at[at, :], sems.at[k])

    for k, part in enumerate(w_in_parts):
        shard_copy(part, w_in, k, in_sem).start()
    for k, part in enumerate(w_out_parts):
        shard_copy(part, w_out, k, out_sem).start()

    slab_copy(own, z, 0).wait()
    slab_copy(near, pair, 1).wait()
    slab_copy(mid_inner, mid, 2).wait()
    slab_copy(far_inner, far, 3).wait()

    step = 64
    gain, shift = gain_ref[...], shift_ref[...]

    def normalize(i, carry):
        at = pl.ds(pl.multiple_of(i * step, step), step)
        values = x[at, :].astype(jnp.float32)
        average = jnp.sum(values, axis=1, keepdims=True) * (1.0 / channels)
        centered = values - average
        variance = jnp.sum(centered * centered, axis=1, keepdims=True) * (1.0 / channels)
        x[at, :] = (centered * lax.rsqrt(variance + EPSILON) * gain + shift).astype(x.dtype)
        return carry

    lax.fori_loop(0, pixels // step, normalize, 0)

    for k, part in enumerate(w_in_parts):
        shard_copy(part, w_in, k, in_sem).wait()
    block = 256
    for f in range(0, units, block):
        pre_act = jnp.dot(x[...], w_in[:, f : f + block], preferred_element_type=jnp.float32)
        pre_act = pre_act + b_in_ref[:, f : f + block]
        gelu = pre_act * (lax.erf(pre_act * (0.5**0.5)) * 0.5 + 0.5)
        hidden[:, f : f + block] = gelu.astype(hidden.dtype)

    for k, part in enumerate(w_out_parts):
        shard_copy(part, w_out, k, out_sem).wait()
    for out_ref, place in zip(out_refs, (far, mid, pair, z), strict=True):
        rows, _, width = out_ref.shape
        at = pl.ds(pl.multiple_of(place * slab, 16), slab)
        partial = lax.dot_general(
            w_out[at, :], hidden[...], (((1,), (1,)), ((), ())), preferred_element_type=jnp.float32
        )
        for row in range(rows):
            out_ref[row] = partial[:, row * width : (row + 1) * width].astype(out_ref.dtype)


def mlp_chunk(slabs, w_in_parts, w_out_parts, gain, shift, b_in):
    rows, width, slab = slabs[0].shape
    shard, units = w_in_parts[0].shape
    channels = shard * len(w_in_parts)
    pixels = rows * width
    anywhere = pl.BlockSpec(memory_space=pl.ANY)
    whole = pl.BlockSpec(memory_space=pltpu.VMEM)
    return pl.pallas_call(
        mlp_kernel,
        in_specs=[anywhere] * (len(slabs) + len(w_in_parts) + len(w_out_parts)) + [whole] * 3,
        out_specs=[whole] * 4,
        out_shape=[jax.ShapeDtypeStruct((rows, slab, width), jnp.bfloat16)] * 4,
        scratch_shapes=[
            pltpu.VMEM((pixels, channels), jnp.bfloat16),
            pltpu.VMEM((channels, units), jnp.bfloat16),
            pltpu.VMEM((channels, units), jnp.bfloat16),
            pltpu.VMEM((pixels, units), jnp.bfloat16),
            pltpu.SemaphoreType.DMA((4,)),
            pltpu.SemaphoreType.DMA((len(w_in_parts),)),
            pltpu.SemaphoreType.DMA((len(w_out_parts),)),
        ],
        compiler_params=pltpu.CompilerParams(vmem_limit_bytes=VMEM_LIMIT),
        cost_estimate=pl.CostEstimate(
            flops=4 * pixels * channels * units,
            bytes_accessed=4 * channels * units + 4 * pixels * channels,
            transcendentals=pixels * units,
        ),
        name="mlp",
    )(
        *[s.reshape(pixels, slab) for s in slabs],
        *w_in_parts,
        *w_out_parts,
        gain[None],
        shift[None],
        b_in[None],
    )


PAIRS = [(0, 1), (1, 0), (2, 3), (3, 2)]
MIDDLE = [(1, 2), (2, 1)]
OUTWARD = [(1, 0), (2, 3)]
INWARD = [(0, 1), (3, 2)]


def gather_line(slab):
    near = lax.ppermute(slab, "chan", PAIRS)
    mid_inner = lax.ppermute(slab, "chan", MIDDLE)
    far_inner = lax.ppermute(near, "chan", MIDDLE)
    mid_outer = lax.ppermute(mid_inner, "chan", OUTWARD)
    far_outer = lax.ppermute(far_inner, "chan", OUTWARD)
    return slab, near, mid_inner, mid_outer, far_inner, far_outer


def add(a, b):
    return (a.astype(jnp.float32) + b.astype(jnp.float32)).astype(jnp.bfloat16)


def scatter_line(far, mid, near, own):
    far_in = lax.ppermute(far, "chan", INWARD)
    mid_in = lax.ppermute(mid, "chan", INWARD)
    far_across = lax.ppermute(add(far, far_in), "chan", MIDDLE)
    mid_across = lax.ppermute(add(mid, mid_in), "chan", MIDDLE)
    from_pair = lax.ppermute(add(near, far_across), "chan", PAIRS)
    return own.astype(jnp.float32) + mid_across.astype(jnp.float32) + from_pair.astype(jnp.float32)


def flipped(array, bit):
    return lax.ppermute(array, "tile", [(i, i ^ bit) for i in range(8)])


def gather_shards(w_in, w_out):
    in_x, in_y = flipped(w_in, 2), flipped(w_in, 4)
    out_x, out_y = flipped(w_out, 2), flipped(w_out, 4)
    in_xy, out_xy = flipped(in_x, 4), flipped(out_y, 2)
    ins, outs = [w_in, in_x, in_y, in_xy], [w_out, out_x, out_y, out_xy]
    ins = [part for mine in ins for part in (mine, flipped(mine, 1))]
    outs = [part for mine in outs for part in (mine, flipped(mine, 1))]
    return ins, outs


def rims(features):
    count = lax.axis_size("tile")
    forward = [(i, i + 1) for i in range(count - 1)]
    backward = [(b, a) for a, b in forward]
    low = lax.ppermute(features[-REACH:], "tile", forward)
    high = lax.ppermute(features[:REACH], "tile", backward)
    return low, high


def local(features, dw_weight, dw_bias, ln_gain, ln_bias, w_in, b_in, w_out, b_out, gamma):
    height = features.shape[0]
    low, high = rims(features)
    taps = jnp.concatenate([dw_weight, dw_bias[:, None]], axis=1)
    w_in_parts, w_out_parts = gather_shards(w_in, w_out.T)
    rows = height // CHUNKS
    results = []
    for first in range(0, height, rows):
        slab = conv_chunk(first, rows, low, features, high, taps)
        partials = mlp_chunk(gather_line(slab), w_in_parts, w_out_parts, ln_gain, ln_bias, b_in)
        projected = scatter_line(*partials) + b_out[None, :, None]
        block = features[first : first + rows].astype(jnp.float32)
        results.append((block + gamma[None, :, None] * projected).astype(jnp.bfloat16))
    return jnp.concatenate(results, axis=0)


def plain(features, dw_weight, dw_bias, ln_gain, ln_bias, w_in, b_in, w_out, b_out, gamma):
    rows, slab, width = features.shape
    low, high = rims(features)
    image = jnp.concatenate([low, features, high], axis=0).astype(jnp.float32)
    image = jnp.pad(image, ((0, 0), (0, 0), (REACH, REACH)))
    total = jnp.zeros((rows, slab, width), jnp.float32) + dw_bias[None, :, None]
    for a in range(SIDE):
        for b in range(SIDE):
            window = image[a : a + rows, :, b : b + width]
            total = total + window * dw_weight[:, a * SIDE + b][None, :, None]
    conv_out = lax.all_gather(total.astype(jnp.bfloat16), "chan", axis=1, tiled=True)
    values = conv_out.astype(jnp.float32)
    centered = values - jnp.mean(values, axis=1, keepdims=True)
    variance = jnp.mean(centered * centered, axis=1, keepdims=True)
    normed = centered * lax.rsqrt(variance + EPSILON) * ln_gain[None, :, None] + ln_bias[None, :, None]
    pre_act = jnp.einsum(
        "rcw,cf->rwf",
        normed.astype(jnp.bfloat16),
        lax.all_gather(w_in, "tile", axis=0, tiled=True),
        preferred_element_type=jnp.float32,
    )
    hidden = jax.nn.gelu(pre_act + b_in[None, None, :], approximate=False).astype(jnp.bfloat16)
    partial = jnp.einsum(
        "rwf,fc->rwc",
        hidden,
        lax.all_gather(w_out, "tile", axis=1, tiled=True),
        preferred_element_type=jnp.float32,
    )
    summed = lax.psum_scatter(
        partial.astype(jnp.bfloat16), "chan", scatter_dimension=2, tiled=True
    ).astype(jnp.float32)
    projected = jnp.transpose(summed + b_out[None, None, :], (0, 2, 1))
    return (features.astype(jnp.float32) + gamma[None, :, None] * projected).astype(jnp.bfloat16)


def solution(mesh):
    placed = (
        P("tile", "chan", None),
        P("chan", None),
        P("chan"),
        P(),
        P(),
        P("tile", "chan"),
        P("chan"),
        P("chan", "tile"),
        P("chan"),
        P("chan"),
    )
    cube = mesh.shape["tile"] == 8 and mesh.shape["chan"] == 4
    return jax.shard_map(
        local if cube else plain,
        mesh=mesh,
        in_specs=placed,
        out_specs=P("tile", "chan", None),
        check_vma=False,
    )
```

```python
import functools

import jax
import jax.numpy as jnp
from jax import lax
from jax.experimental import pallas as pl
from jax.experimental.pallas import tpu as pltpu
from jax.sharding import PartitionSpec as P

SIDE = 7
REACH = SIDE // 2
CHUNKS = 2
VMEM_LIMIT = 48 * 1024 * 1024
EPSILON = 1e-06


def conv_kernel(plan, *refs):
    sources, taps_ref, bias_ref, out_ref, image = refs[:-4], *refs[-4:]
    rows, width, channels = out_ref.shape
    edge = (image.shape[1] - width) // 2
    blank = jnp.zeros((edge, channels), jnp.float32)
    for i, (source, row) in enumerate(plan):
        image[i, :edge, :] = blank
        image[i, edge + width :, :] = blank
        image[i, edge : edge + width, :] = sources[source][row].astype(jnp.float32).T
    bias = bias_ref[...]
    tile = 16

    def one_tile(i, carry):
        start = pl.multiple_of(i * tile, tile)
        totals = [jnp.broadcast_to(bias, (tile, channels)) for _ in range(rows)]
        for b in range(SIDE):
            for j in range(len(plan)):
                pixels = image[j, pl.ds(start + (edge - REACH + b), tile), :]
                for row in range(rows):
                    a = j - row
                    if 0 <= a < SIDE:
                        tap = SIDE * a + b
                        totals[row] = totals[row] + pixels * taps_ref[tap : tap + 1, :]
        for row in range(rows):
            out_ref[row, pl.ds(start, tile), :] = totals[row].astype(out_ref.dtype)
        return carry

    lax.fori_loop(0, width // tile, one_tile, 0)


def conv_chunk(first, rows, low, features, high, taps, bias):
    height, slab, width = features.shape
    names, plan = ["features"], []
    for row in range(first - REACH, first + rows + REACH):
        if row < 0:
            name, index = "low", row + REACH
        elif row < height:
            name, index = "features", row
        else:
            name, index = "high", row - height
        if name not in names:
            names.append(name)
        plan.append((names.index(name), index))
    arrays = [{"features": features, "low": low, "high": high}[name] for name in names]
    block = 128
    return pl.pallas_call(
        functools.partial(conv_kernel, tuple(plan)),
        grid=(slab // block,),
        in_specs=[pl.BlockSpec((a.shape[0], block, width), lambda i: (0, i, 0)) for a in arrays]
        + [pl.BlockSpec((t.shape[0], block), lambda i: (0, i)) for t in (taps, bias)],
        out_specs=pl.BlockSpec((rows, width, block), lambda i: (0, 0, i)),
        out_shape=jax.ShapeDtypeStruct((rows, width, slab), jnp.bfloat16),
        scratch_shapes=[pltpu.VMEM((len(plan), width + 16, block), jnp.float32)],
        compiler_params=pltpu.CompilerParams(vmem_limit_bytes=VMEM_LIMIT),
        cost_estimate=pl.CostEstimate(
            flops=2 * SIDE * SIDE * rows * slab * width,
            bytes_accessed=4 * rows * slab * width,
            transcendentals=0,
        ),
        name="depthwise",
    )(*arrays, taps, bias)


def line_places(z):
    low_half = z < 2
    return z ^ 1, jnp.where(low_half, 2, 1), jnp.where(low_half, 3, 0)


def mlp_kernel(*refs):
    own, near, mid_inner, mid_outer, far_inner, far_outer = refs[:6]
    w_in_parts, w_out_parts = refs[6:14], refs[14:22]
    gain_ref, shift_ref, b_in_ref = refs[22:25]
    out_refs = refs[25:29]
    x, w_in, w_out, hidden, x_sem, in_sem, out_sem = refs[29:]
    pixels, channels = x.shape
    slab = own.shape[1]
    units = hidden.shape[1]
    shard = w_in_parts[0].shape[0]
    z, t = lax.axis_index("chan"), lax.axis_index("tile")
    pair, mid, far = line_places(z)
    inner = jnp.logical_or(z == 1, z == 2)

    def slab_copy(part, place, sem):
        at = pl.ds(pl.multiple_of(place * slab, 128), slab)
        return pltpu.make_async_copy(part, x.at[:, at], x_sem.at[sem])

    slab_copy(own, z, 0).start()
    slab_copy(near, pair, 1).start()

    @pl.when(inner)
    def _():
        slab_copy(mid_inner, mid, 2).start()
        slab_copy(far_inner, far, 3).start()

    @pl.when(jnp.logical_not(inner))
    def _():
        slab_copy(mid_outer, mid, 2).start()
        slab_copy(far_outer, far, 3).start()

    def shard_copy(part, target, k, sems):
        at = pl.ds(pl.multiple_of((t ^ k) * shard, 16), shard)
        return pltpu.make_async_copy(part, target.at[at, :], sems.at[k])

    for k, part in enumerate(w_in_parts):
        shard_copy(part, w_in, k, in_sem).start()
    for k, part in enumerate(w_out_parts):
        shard_copy(part, w_out, k, out_sem).start()

    slab_copy(own, z, 0).wait()
    slab_copy(near, pair, 1).wait()
    slab_copy(mid_inner, mid, 2).wait()
    slab_copy(far_inner, far, 3).wait()

    step = 64
    gain, shift = gain_ref[...], shift_ref[...]

    def normalize(i, carry):
        at = pl.ds(pl.multiple_of(i * step, step), step)
        values = x[at, :].astype(jnp.float32)
        average = jnp.sum(values, axis=1, keepdims=True) * (1.0 / channels)
        centered = values - average
        variance = jnp.sum(centered * centered, axis=1, keepdims=True) * (1.0 / channels)
        x[at, :] = (centered * lax.rsqrt(variance + EPSILON) * gain + shift).astype(x.dtype)
        return carry

    lax.fori_loop(0, pixels // step, normalize, 0)

    for k, part in enumerate(w_in_parts):
        shard_copy(part, w_in, k, in_sem).wait()
    block = 256
    for f in range(0, units, block):
        pre_act = jnp.dot(x[...], w_in[:, f : f + block], preferred_element_type=jnp.float32)
        pre_act = pre_act + b_in_ref[:, f : f + block]
        gelu = pre_act * (lax.erf(pre_act * (0.5**0.5)) * 0.5 + 0.5)
        hidden[:, f : f + block] = gelu.astype(hidden.dtype)

    for k, part in enumerate(w_out_parts):
        shard_copy(part, w_out, k, out_sem).wait()
    for out_ref, place in zip(out_refs, (far, mid, pair, z), strict=True):
        rows, _, width = out_ref.shape
        at = pl.ds(pl.multiple_of(place * slab, 16), slab)
        partial = lax.dot_general(
            w_out[at, :], hidden[...], (((1,), (1,)), ((), ())), preferred_element_type=jnp.float32
        )
        for row in range(rows):
            out_ref[row] = partial[:, row * width : (row + 1) * width].astype(out_ref.dtype)


def mlp_chunk(slabs, w_in_parts, w_out_parts, gain, shift, b_in):
    rows, width, slab = slabs[0].shape
    shard, units = w_in_parts[0].shape
    channels = shard * len(w_in_parts)
    pixels = rows * width
    anywhere = pl.BlockSpec(memory_space=pl.ANY)
    whole = pl.BlockSpec(memory_space=pltpu.VMEM)
    return pl.pallas_call(
        mlp_kernel,
        in_specs=[anywhere] * (len(slabs) + len(w_in_parts) + len(w_out_parts)) + [whole] * 3,
        out_specs=[whole] * 4,
        out_shape=[jax.ShapeDtypeStruct((rows, slab, width), jnp.bfloat16)] * 4,
        scratch_shapes=[
            pltpu.VMEM((pixels, channels), jnp.bfloat16),
            pltpu.VMEM((channels, units), jnp.bfloat16),
            pltpu.VMEM((channels, units), jnp.bfloat16),
            pltpu.VMEM((pixels, units), jnp.bfloat16),
            pltpu.SemaphoreType.DMA((4,)),
            pltpu.SemaphoreType.DMA((len(w_in_parts),)),
            pltpu.SemaphoreType.DMA((len(w_out_parts),)),
        ],
        compiler_params=pltpu.CompilerParams(vmem_limit_bytes=VMEM_LIMIT),
        cost_estimate=pl.CostEstimate(
            flops=4 * pixels * channels * units,
            bytes_accessed=4 * channels * units + 4 * pixels * channels,
            transcendentals=pixels * units,
        ),
        name="mlp",
    )(
        *[s.reshape(pixels, slab) for s in slabs],
        *w_in_parts,
        *w_out_parts,
        gain[None],
        shift[None],
        b_in[None],
    )


PAIRS = [(0, 1), (1, 0), (2, 3), (3, 2)]
MIDDLE = [(1, 2), (2, 1)]
OUTWARD = [(1, 0), (2, 3)]
INWARD = [(0, 1), (3, 2)]


def gather_line(slab):
    near = lax.ppermute(slab, "chan", PAIRS)
    mid_inner = lax.ppermute(slab, "chan", MIDDLE)
    far_inner = lax.ppermute(near, "chan", MIDDLE)
    mid_outer = lax.ppermute(mid_inner, "chan", OUTWARD)
    far_outer = lax.ppermute(far_inner, "chan", OUTWARD)
    return slab, near, mid_inner, mid_outer, far_inner, far_outer


def add(a, b):
    return (a.astype(jnp.float32) + b.astype(jnp.float32)).astype(jnp.bfloat16)


def scatter_line(far, mid, near, own):
    far_in = lax.ppermute(far, "chan", INWARD)
    mid_in = lax.ppermute(mid, "chan", INWARD)
    far_across = lax.ppermute(add(far, far_in), "chan", MIDDLE)
    mid_across = lax.ppermute(add(mid, mid_in), "chan", MIDDLE)
    from_pair = lax.ppermute(add(near, far_across), "chan", PAIRS)
    return own.astype(jnp.float32) + mid_across.astype(jnp.float32) + from_pair.astype(jnp.float32)


def flipped(array, bit):
    return lax.ppermute(array, "tile", [(i, i ^ bit) for i in range(8)])


def gather_shards(w_in, w_out):
    in_x, in_y = flipped(w_in, 2), flipped(w_in, 4)
    out_x, out_y = flipped(w_out, 2), flipped(w_out, 4)
    in_xy, out_xy = flipped(in_x, 4), flipped(out_y, 2)
    ins, outs = [w_in, in_x, in_y, in_xy], [w_out, out_x, out_y, out_xy]
    ins = [part for mine in ins for part in (mine, flipped(mine, 1))]
    outs = [part for mine in outs for part in (mine, flipped(mine, 1))]
    return ins, outs


def rims(features):
    count = lax.axis_size("tile")
    forward = [(i, i + 1) for i in range(count - 1)]
    backward = [(b, a) for a, b in forward]
    low = lax.ppermute(features[-REACH:], "tile", forward)
    high = lax.ppermute(features[:REACH], "tile", backward)
    return low, high


def local(features, dw_weight, dw_bias, ln_gain, ln_bias, w_in, b_in, w_out, b_out, gamma):
    height = features.shape[0]
    low, high = rims(features)
    w_in_parts, w_out_parts = gather_shards(w_in, w_out.T)
    rows = height // CHUNKS
    results = []
    for first in range(0, height, rows):
        slab = conv_chunk(first, rows, low, features, high, dw_weight.T, dw_bias[None])
        partials = mlp_chunk(gather_line(slab), w_in_parts, w_out_parts, ln_gain, ln_bias, b_in)
        projected = scatter_line(*partials) + b_out[None, :, None]
        block = features[first : first + rows].astype(jnp.float32)
        results.append((block + gamma[None, :, None] * projected).astype(jnp.bfloat16))
    return jnp.concatenate(results, axis=0)


def plain(features, dw_weight, dw_bias, ln_gain, ln_bias, w_in, b_in, w_out, b_out, gamma):
    rows, slab, width = features.shape
    low, high = rims(features)
    image = jnp.concatenate([low, features, high], axis=0).astype(jnp.float32)
    image = jnp.pad(image, ((0, 0), (0, 0), (REACH, REACH)))
    total = jnp.zeros((rows, slab, width), jnp.float32) + dw_bias[None, :, None]
    for a in range(SIDE):
        for b in range(SIDE):
            window = image[a : a + rows, :, b : b + width]
            total = total + window * dw_weight[:, a * SIDE + b][None, :, None]
    conv_out = lax.all_gather(total.astype(jnp.bfloat16), "chan", axis=1, tiled=True)
    values = conv_out.astype(jnp.float32)
    centered = values - jnp.mean(values, axis=1, keepdims=True)
    variance = jnp.mean(centered * centered, axis=1, keepdims=True)
    normed = centered * lax.rsqrt(variance + EPSILON) * ln_gain[None, :, None] + ln_bias[None, :, None]
    pre_act = jnp.einsum(
        "rcw,cf->rwf",
        normed.astype(jnp.bfloat16),
        lax.all_gather(w_in, "tile", axis=0, tiled=True),
        preferred_element_type=jnp.float32,
    )
    hidden = jax.nn.gelu(pre_act + b_in[None, None, :], approximate=False).astype(jnp.bfloat16)
    partial = jnp.einsum(
        "rwf,fc->rwc",
        hidden,
        lax.all_gather(w_out, "tile", axis=1, tiled=True),
        preferred_element_type=jnp.float32,
    )
    summed = lax.psum_scatter(
        partial.astype(jnp.bfloat16), "chan", scatter_dimension=2, tiled=True
    ).astype(jnp.float32)
    projected = jnp.transpose(summed + b_out[None, None, :], (0, 2, 1))
    return (features.astype(jnp.float32) + gamma[None, :, None] * projected).astype(jnp.bfloat16)


def solution(mesh):
    placed = (
        P("tile", "chan", None),
        P("chan", None),
        P("chan"),
        P(),
        P(),
        P("tile", "chan"),
        P("chan"),
        P("chan", "tile"),
        P("chan"),
        P("chan"),
    )
    cube = mesh.shape["tile"] == 8 and mesh.shape["chan"] == 4
    return jax.shard_map(
        local if cube else plain,
        mesh=mesh,
        in_specs=placed,
        out_specs=P("tile", "chan", None),
        check_vma=False,
    )
```

```python
import functools

import jax
import jax.numpy as jnp
from jax import lax
from jax.experimental import pallas as pl
from jax.experimental.pallas import tpu as pltpu
from jax.sharding import PartitionSpec as P

SIDE = 7
REACH = SIDE // 2
VMEM_LIMIT = 48 * 1024 * 1024
EPSILON = 1e-06


def conv_kernel(plan, *refs):
    sources, taps_ref, bias_ref, out_ref, image = refs[:-4], *refs[-4:]
    rows, width, channels = out_ref.shape
    edge = (image.shape[1] - width) // 2
    blank = jnp.zeros((edge, channels), jnp.float32)
    for i, (source, row) in enumerate(plan):
        image[i, :edge, :] = blank
        image[i, edge + width :, :] = blank
        image[i, edge : edge + width, :] = sources[source][row].astype(jnp.float32).T
    bias = bias_ref[...]
    tile = 16

    def one_tile(i, carry):
        start = pl.multiple_of(i * tile, tile)
        totals = [jnp.broadcast_to(bias, (tile, channels)) for _ in range(rows)]
        for b in range(SIDE):
            for j in range(len(plan)):
                pixels = image[j, pl.ds(start + (edge - REACH + b), tile), :]
                for row in range(rows):
                    a = j - row
                    if 0 <= a < SIDE:
                        tap = SIDE * a + b
                        totals[row] = totals[row] + pixels * taps_ref[tap : tap + 1, :]
        for row in range(rows):
            out_ref[row, pl.ds(start, tile), :] = totals[row].astype(out_ref.dtype)
        return carry

    lax.fori_loop(0, width // tile, one_tile, 0)


def conv_chunk(first, rows, *, low, features, high, taps, bias):
    height, slab, width = features.shape
    names, plan = ["features"], []
    for row in range(first - REACH, first + rows + REACH):
        if row < 0:
            name, index = "low", row + REACH
        elif row < height:
            name, index = "features", row
        else:
            name, index = "high", row - height
        if name not in names:
            names.append(name)
        plan.append((names.index(name), index))
    arrays = [{"features": features, "low": low, "high": high}[name] for name in names]
    block = 128
    return pl.pallas_call(
        functools.partial(conv_kernel, tuple(plan)),
        grid=(slab // block,),
        in_specs=[pl.BlockSpec((a.shape[0], block, width), lambda i: (0, i, 0)) for a in arrays]
        + [pl.BlockSpec((t.shape[0], block), lambda i: (0, i)) for t in (taps, bias)],
        out_specs=pl.BlockSpec((rows, width, block), lambda i: (0, 0, i)),
        out_shape=jax.ShapeDtypeStruct((rows, width, slab), jnp.bfloat16),
        scratch_shapes=[pltpu.VMEM((len(plan), width + 16, block), jnp.float32)],
        compiler_params=pltpu.CompilerParams(vmem_limit_bytes=VMEM_LIMIT),
        cost_estimate=pl.CostEstimate(
            flops=2 * SIDE * SIDE * rows * slab * width,
            bytes_accessed=4 * rows * slab * width,
            transcendentals=0,
        ),
        name="depthwise",
    )(*arrays, taps, bias)


def line_places(z):
    low_half = z < 2
    return z ^ 1, jnp.where(low_half, 2, 1), jnp.where(low_half, 3, 0)


def weight_pieces(parts, shard):
    own, x, y, in_xy, out_xy, others, other_xy = parts
    three = [(own, 0), (x, 2), (y, 4)]
    ins = [(part, 0, k) for part, k in three] + [(in_xy, 0, 6), (other_xy, 0, 7)]
    outs = [(part, shard, k) for part, k in three] + [(out_xy, 0, 6), (other_xy, shard, 7)]
    for i, k in enumerate((1, 3, 5)):
        ins.append((others, 2 * shard * i, k))
        outs.append((others, 2 * shard * i + shard, k))
    return ins, outs


def mlp_kernel(*refs):
    own, near, mid_inner, mid_outer, far_inner, far_outer = refs[:6]
    refs = refs[6:]
    parts, refs = refs[: len(refs) - 14], refs[len(refs) - 14 :]
    shard = parts[0].shape[0] // 2
    w_in_parts, w_out_parts = weight_pieces(parts, shard)
    gain_ref, shift_ref, b_in_ref = refs[:3]
    out_refs = refs[3:7]
    x, w_in, w_out, hidden, x_sem, in_sem, out_sem = refs[7:]
    pixels, channels = x.shape
    slab = own.shape[1]
    units = hidden.shape[1]
    z, t = lax.axis_index("chan"), lax.axis_index("tile")
    pair, mid, far = line_places(z)
    inner = jnp.logical_or(z == 1, z == 2)

    def slab_copy(part, place, sem):
        at = pl.ds(pl.multiple_of(place * slab, 128), slab)
        return pltpu.make_async_copy(part, x.at[:, at], x_sem.at[sem])

    slab_copy(own, z, 0).start()
    slab_copy(near, pair, 1).start()

    @pl.when(inner)
    def _():
        slab_copy(mid_inner, mid, 2).start()
        slab_copy(far_inner, far, 3).start()

    @pl.when(jnp.logical_not(inner))
    def _():
        slab_copy(mid_outer, mid, 2).start()
        slab_copy(far_outer, far, 3).start()

    def shard_copy(piece, target, sems):
        part, first, k = piece
        at = pl.ds(pl.multiple_of((t ^ k) * shard, 16), shard)
        return pltpu.make_async_copy(part.at[first : first + shard, :], target.at[at, :], sems.at[k])

    for piece in w_in_parts:
        shard_copy(piece, w_in, in_sem).start()
    for piece in w_out_parts:
        shard_copy(piece, w_out, out_sem).start()

    slab_copy(own, z, 0).wait()
    slab_copy(near, pair, 1).wait()
    slab_copy(mid_inner, mid, 2).wait()
    slab_copy(far_inner, far, 3).wait()

    step = 64
    gain, shift = gain_ref[...], shift_ref[...]

    def normalize(i, carry):
        at = pl.ds(pl.multiple_of(i * step, step), step)
        values = x[at, :].astype(jnp.float32)
        average = jnp.sum(values, axis=1, keepdims=True) * (1.0 / channels)
        centered = values - average
        variance = jnp.sum(centered * centered, axis=1, keepdims=True) * (1.0 / channels)
        x[at, :] = (centered * lax.rsqrt(variance + EPSILON) * gain + shift).astype(x.dtype)
        return carry

    lax.fori_loop(0, pixels // step, normalize, 0)

    for piece in w_in_parts:
        shard_copy(piece, w_in, in_sem).wait()
    block = 256
    for f in range(0, units, block):
        pre_act = jnp.dot(x[...], w_in[:, f : f + block], preferred_element_type=jnp.float32)
        pre_act = pre_act + b_in_ref[:, f : f + block]
        gelu = pre_act * (lax.erf(pre_act * (0.5**0.5)) * 0.5 + 0.5)
        hidden[:, f : f + block] = gelu.astype(hidden.dtype)

    for piece in w_out_parts:
        shard_copy(piece, w_out, out_sem).wait()
    for out_ref, place in zip(out_refs, (far, mid, pair, z), strict=True):
        rows, _, width = out_ref.shape
        at = pl.ds(pl.multiple_of(place * slab, 16), slab)
        partial = lax.dot_general(
            w_out[at, :], hidden[...], (((1,), (1,)), ((), ())), preferred_element_type=jnp.float32
        )
        for row in range(rows):
            out_ref[row] = partial[:, row * width : (row + 1) * width].astype(out_ref.dtype)


def mlp_chunk(slabs, weights, gain, shift, b_in):
    rows, width, slab = slabs[0].shape
    shards = 8
    units = weights[0].shape[1]
    channels = slab * 4
    pixels = rows * width
    anywhere = pl.BlockSpec(memory_space=pl.ANY)
    whole = pl.BlockSpec(memory_space=pltpu.VMEM)
    return pl.pallas_call(
        mlp_kernel,
        in_specs=[anywhere] * (len(slabs) + len(weights)) + [whole] * 3,
        out_specs=[whole] * 4,
        out_shape=[jax.ShapeDtypeStruct((rows, slab, width), jnp.bfloat16)] * 4,
        scratch_shapes=[
            pltpu.VMEM((pixels, channels), jnp.bfloat16),
            pltpu.VMEM((channels, units), jnp.bfloat16),
            pltpu.VMEM((channels, units), jnp.bfloat16),
            pltpu.VMEM((pixels, units), jnp.bfloat16),
            pltpu.SemaphoreType.DMA((4,)),
            pltpu.SemaphoreType.DMA((shards,)),
            pltpu.SemaphoreType.DMA((shards,)),
        ],
        compiler_params=pltpu.CompilerParams(vmem_limit_bytes=28 * 1024 * 1024),
        cost_estimate=pl.CostEstimate(
            flops=4 * pixels * channels * units,
            bytes_accessed=4 * channels * units + 4 * pixels * channels,
            transcendentals=pixels * units,
        ),
        name="mlp",
    )(
        *[s.reshape(pixels, slab) for s in slabs],
        *weights,
        gain[None],
        shift[None],
        b_in[None],
    )


def to_pair(array):
    return lax.ppermute(array, "chan", [(0, 1), (1, 0), (2, 3), (3, 2)])


def to_middle(array):
    return lax.ppermute(array, "chan", [(1, 2), (2, 1)])


def outward(array):
    return lax.ppermute(array, "chan", [(1, 0), (2, 3)])


def inward(array):
    return lax.ppermute(array, "chan", [(0, 1), (3, 2)])


def after(value, *others):
    return lax.optimization_barrier((value, *others))[0] if others else value


def add(a, b):
    return (a.astype(jnp.float32) + b.astype(jnp.float32)).astype(jnp.bfloat16)


def flipped(array, bit):
    return lax.ppermute(array, "tile", [(i, i ^ bit) for i in range(8)])


def rims(top, bottom):
    count = lax.axis_size("tile")
    forward = [(i, i + 1) for i in range(count - 1)]
    backward = [(b, a) for a, b in forward]
    return lax.ppermute(bottom, "tile", forward), lax.ppermute(top, "tile", backward)


def local(features, dw_weight, dw_bias, ln_gain, ln_bias, w_in, b_in, w_out, b_out, gamma):
    height = features.shape[0]
    rows = height // 2
    shard = w_in.shape[0]
    conv = functools.partial(conv_chunk, features=features, taps=dw_weight.T, bias=dw_bias[None])
    mlp = functools.partial(mlp_chunk, gain=ln_gain, shift=ln_bias, b_in=b_in)

    low, high = rims(features[:REACH], features[-REACH:])
    slab_0 = conv(0, rows, low=low, high=high)
    slab_1 = conv(rows, rows, low=low, high=high)

    own = jnp.concatenate([w_in, w_out.T], axis=0)
    moving = after(own, low, high)
    own_x, own_y = flipped(moving, 2), flipped(moving, 4)

    near_0, mid_in_0 = to_pair(slab_0), to_middle(slab_0)
    far_in_0, mid_out_0 = to_middle(near_0), outward(mid_in_0)
    far_out_0 = outward(far_in_0)

    begun = own_x, own_y, far_in_0, mid_out_0, slab_1
    in_xy = flipped(after(own_x, *begun)[:shard], 4)
    out_xy = flipped(after(own_y, *begun)[shard:], 2)
    near_1, mid_in_1 = to_pair(after(slab_1, *begun)), to_middle(after(slab_1, *begun))

    ready = in_xy, out_xy, far_out_0, near_1, mid_in_1
    others = flipped(after(jnp.concatenate([own, own_x, own_y], axis=0), *ready), 1)
    other_xy = flipped(after(jnp.concatenate([in_xy, out_xy], axis=0), *ready), 1)
    far_in_1, mid_out_1 = to_middle(after(near_1, *ready)), outward(after(mid_in_1, *ready))
    weights = [own, own_x, own_y, in_xy, out_xy, others, other_xy]

    line_0 = [slab_0, near_0, mid_in_0, mid_out_0, far_in_0, far_out_0]
    far_0, mid_0, pair_0, home_0 = mlp(line_0, weights)
    far_out_1 = outward(after(far_in_1, far_0))
    far_sum_0, mid_from_0 = add(far_0, inward(far_0)), inward(mid_0)

    line_1 = [slab_1, near_1, mid_in_1, mid_out_1, far_in_1, far_out_1]
    far_1, mid_1, pair_1, home_1 = mlp(line_1, weights)

    far_across_0 = to_middle(far_sum_0)
    mid_across_0 = to_middle(add(mid_0, mid_from_0))
    from_pair_0 = to_pair(add(pair_0, far_across_0))

    far_sum_1, mid_from_1 = add(far_1, inward(far_1)), inward(mid_1)
    far_across_1 = to_middle(far_sum_1)
    mid_across_1 = to_middle(add(mid_1, mid_from_1))
    from_pair_1 = to_pair(add(pair_1, far_across_1))

    results = []
    for first, parts in (
        (0, (home_0, mid_across_0, from_pair_0)),
        (rows, (home_1, mid_across_1, from_pair_1)),
    ):
        projected = sum(part.astype(jnp.float32) for part in parts) + b_out[None, :, None]
        block = features[first : first + rows].astype(jnp.float32)
        results.append((block + gamma[None, :, None] * projected).astype(jnp.bfloat16))
    return jnp.concatenate(results, axis=0)


def plain(features, dw_weight, dw_bias, ln_gain, ln_bias, w_in, b_in, w_out, b_out, gamma):
    rows, slab, width = features.shape
    low, high = rims(features[:REACH], features[-REACH:])
    image = jnp.concatenate([low, features, high], axis=0).astype(jnp.float32)
    image = jnp.pad(image, ((0, 0), (0, 0), (REACH, REACH)))
    total = jnp.zeros((rows, slab, width), jnp.float32) + dw_bias[None, :, None]
    for a in range(SIDE):
        for b in range(SIDE):
            window = image[a : a + rows, :, b : b + width]
            total = total + window * dw_weight[:, a * SIDE + b][None, :, None]
    conv_out = lax.all_gather(total.astype(jnp.bfloat16), "chan", axis=1, tiled=True)
    values = conv_out.astype(jnp.float32)
    centered = values - jnp.mean(values, axis=1, keepdims=True)
    variance = jnp.mean(centered * centered, axis=1, keepdims=True)
    normed = centered * lax.rsqrt(variance + EPSILON) * ln_gain[None, :, None] + ln_bias[None, :, None]
    pre_act = jnp.einsum(
        "rcw,cf->rwf",
        normed.astype(jnp.bfloat16),
        lax.all_gather(w_in, "tile", axis=0, tiled=True),
        preferred_element_type=jnp.float32,
    )
    hidden = jax.nn.gelu(pre_act + b_in[None, None, :], approximate=False).astype(jnp.bfloat16)
    partial = jnp.einsum(
        "rwf,fc->rwc",
        hidden,
        lax.all_gather(w_out, "tile", axis=1, tiled=True),
        preferred_element_type=jnp.float32,
    )
    summed = lax.psum_scatter(
        partial.astype(jnp.bfloat16), "chan", scatter_dimension=2, tiled=True
    ).astype(jnp.float32)
    projected = jnp.transpose(summed + b_out[None, None, :], (0, 2, 1))
    return (features.astype(jnp.float32) + gamma[None, :, None] * projected).astype(jnp.bfloat16)


def solution(mesh):
    placed = (
        P("tile", "chan", None),
        P("chan", None),
        P("chan"),
        P(),
        P(),
        P("tile", "chan"),
        P("chan"),
        P("chan", "tile"),
        P("chan"),
        P("chan"),
    )
    cube = mesh.shape["tile"] == 8 and mesh.shape["chan"] == 4
    return jax.shard_map(
        local if cube else plain,
        mesh=mesh,
        in_specs=placed,
        out_specs=P("tile", "chan", None),
        check_vma=False,
    )
```

```python
import functools

import jax
import jax.numpy as jnp
from jax import lax
from jax.experimental import pallas as pl
from jax.experimental.pallas import tpu as pltpu
from jax.sharding import PartitionSpec as P

SIDE = 7
REACH = SIDE // 2
VMEM_LIMIT = 48 * 1024 * 1024
EPSILON = 1e-06


def conv_kernel(plan, *refs):
    sources, taps_ref, bias_ref, out_ref, image = refs[:-4], *refs[-4:]
    rows, width, channels = out_ref.shape
    edge = (image.shape[1] - width) // 2
    blank = jnp.zeros((edge, channels), jnp.float32)
    for i, (source, row) in enumerate(plan):
        image[i, :edge, :] = blank
        image[i, edge + width :, :] = blank
        image[i, edge : edge + width, :] = sources[source][row].astype(jnp.float32).T
    bias = bias_ref[...]
    tile = 16

    def one_tile(i, carry):
        start = pl.multiple_of(i * tile, tile)
        totals = [jnp.broadcast_to(bias, (tile, channels)) for _ in range(rows)]
        for b in range(SIDE):
            for j in range(len(plan)):
                pixels = image[j, pl.ds(start + (edge - REACH + b), tile), :]
                for row in range(rows):
                    a = j - row
                    if 0 <= a < SIDE:
                        tap = SIDE * a + b
                        totals[row] = totals[row] + pixels * taps_ref[tap : tap + 1, :]
        for row in range(rows):
            out_ref[row, pl.ds(start, tile), :] = totals[row].astype(out_ref.dtype)
        return carry

    lax.fori_loop(0, width // tile, one_tile, 0)


def conv_chunk(first, rows, *, low, features, high, taps, bias):
    height, slab, width = features.shape
    names, plan = ["features"], []
    for row in range(first - REACH, first + rows + REACH):
        if row < 0:
            name, index = "low", row + REACH
        elif row < height:
            name, index = "features", row
        else:
            name, index = "high", row - height
        if name not in names:
            names.append(name)
        plan.append((names.index(name), index))
    arrays = [{"features": features, "low": low, "high": high}[name] for name in names]
    block = 128
    return pl.pallas_call(
        functools.partial(conv_kernel, tuple(plan)),
        grid=(slab // block,),
        in_specs=[pl.BlockSpec((a.shape[0], block, width), lambda i: (0, i, 0)) for a in arrays]
        + [pl.BlockSpec((t.shape[0], block), lambda i: (0, i)) for t in (taps, bias)],
        out_specs=pl.BlockSpec((rows, width, block), lambda i: (0, 0, i)),
        out_shape=jax.ShapeDtypeStruct((rows, width, slab), jnp.bfloat16),
        scratch_shapes=[pltpu.VMEM((len(plan), width + 16, block), jnp.float32)],
        compiler_params=pltpu.CompilerParams(vmem_limit_bytes=VMEM_LIMIT),
        cost_estimate=pl.CostEstimate(
            flops=2 * SIDE * SIDE * rows * slab * width,
            bytes_accessed=4 * rows * slab * width,
            transcendentals=0,
        ),
        name="depthwise",
    )(*arrays, taps, bias)


def line_places(z):
    low_half = z < 2
    return z ^ 1, jnp.where(low_half, 2, 1), jnp.where(low_half, 3, 0)


def weight_pieces(parts, shard):
    own, x, y, in_xy, out_xy, others, other_xy = parts
    three = [(own, 0), (x, 2), (y, 4)]
    ins = [(part, 0, k) for part, k in three] + [(in_xy, 0, 6), (other_xy, 0, 7)]
    outs = [(part, shard, k) for part, k in three] + [(out_xy, 0, 6), (other_xy, shard, 7)]
    for i, k in enumerate((1, 3, 5)):
        ins.append((others, 2 * shard * i, k))
        outs.append((others, 2 * shard * i + shard, k))
    return ins, outs


def mlp_kernel(*refs):
    own, near, mid_inner, mid_outer, far_inner, far_outer = refs[:6]
    refs = refs[6:]
    parts, refs = refs[: len(refs) - 14], refs[len(refs) - 14 :]
    shard = parts[0].shape[0] // 2
    w_in_parts, w_out_parts = weight_pieces(parts, shard)
    gain_ref, shift_ref, b_in_ref = refs[:3]
    out_refs = refs[3:7]
    x, w_in, w_out, hidden, x_sem, in_sem, out_sem = refs[7:]
    pixels, channels = x.shape
    slab = own.shape[1]
    units = hidden.shape[1]
    z, t = lax.axis_index("chan"), lax.axis_index("tile")
    pair, mid, far = line_places(z)
    inner = jnp.logical_or(z == 1, z == 2)

    def slab_copy(part, place, sem):
        at = pl.ds(pl.multiple_of(place * slab, 128), slab)
        return pltpu.make_async_copy(part, x.at[:, at], x_sem.at[sem])

    slab_copy(own, z, 0).start()
    slab_copy(near, pair, 1).start()

    @pl.when(inner)
    def _():
        slab_copy(mid_inner, mid, 2).start()
        slab_copy(far_inner, far, 3).start()

    @pl.when(jnp.logical_not(inner))
    def _():
        slab_copy(mid_outer, mid, 2).start()
        slab_copy(far_outer, far, 3).start()

    def shard_copy(piece, target, sems):
        part, first, k = piece
        at = pl.ds(pl.multiple_of((t ^ k) * shard, 16), shard)
        return pltpu.make_async_copy(part.at[first : first + shard, :], target.at[at, :], sems.at[k])

    for piece in w_in_parts:
        shard_copy(piece, w_in, in_sem).start()
    for piece in w_out_parts:
        shard_copy(piece, w_out, out_sem).start()

    slab_copy(own, z, 0).wait()
    slab_copy(near, pair, 1).wait()
    slab_copy(mid_inner, mid, 2).wait()
    slab_copy(far_inner, far, 3).wait()

    step = 256
    gain, shift = gain_ref[...], shift_ref[...]

    def normalize(i, carry):
        at = pl.ds(pl.multiple_of(i * step, step), step)
        values = x[at, :].astype(jnp.float32)
        average = jnp.sum(values, axis=1, keepdims=True) * (1.0 / channels)
        centered = values - average
        variance = jnp.sum(centered * centered, axis=1, keepdims=True) * (1.0 / channels)
        x[at, :] = (centered * lax.rsqrt(variance + EPSILON) * gain + shift).astype(x.dtype)
        return carry

    lax.fori_loop(0, pixels // step, normalize, 0)

    for piece in w_in_parts:
        shard_copy(piece, w_in, in_sem).wait()
    block = 256
    for f in range(0, units, block):
        pre_act = jnp.dot(x[...], w_in[:, f : f + block], preferred_element_type=jnp.float32)
        pre_act = pre_act + b_in_ref[:, f : f + block]
        gelu = pre_act * (lax.erf(pre_act * (0.5**0.5)) * 0.5 + 0.5)
        hidden[:, f : f + block] = gelu.astype(hidden.dtype)

    for piece in w_out_parts:
        shard_copy(piece, w_out, out_sem).wait()
    for out_ref, place in zip(out_refs, (far, mid, pair, z), strict=True):
        rows, _, width = out_ref.shape
        at = pl.ds(pl.multiple_of(place * slab, 16), slab)
        partial = lax.dot_general(
            w_out[at, :], hidden[...], (((1,), (1,)), ((), ())), preferred_element_type=jnp.float32
        )
        for row in range(rows):
            out_ref[row] = partial[:, row * width : (row + 1) * width].astype(out_ref.dtype)


def mlp_chunk(slabs, weights, gain, shift, b_in):
    rows, width, slab = slabs[0].shape
    shards = 8
    units = weights[0].shape[1]
    channels = slab * 4
    pixels = rows * width
    anywhere = pl.BlockSpec(memory_space=pl.ANY)
    whole = pl.BlockSpec(memory_space=pltpu.VMEM)
    return pl.pallas_call(
        mlp_kernel,
        in_specs=[anywhere] * (len(slabs) + len(weights)) + [whole] * 3,
        out_specs=[whole] * 4,
        out_shape=[jax.ShapeDtypeStruct((rows, slab, width), jnp.bfloat16)] * 4,
        scratch_shapes=[
            pltpu.VMEM((pixels, channels), jnp.bfloat16),
            pltpu.VMEM((channels, units), jnp.bfloat16),
            pltpu.VMEM((channels, units), jnp.bfloat16),
            pltpu.VMEM((pixels, units), jnp.bfloat16),
            pltpu.SemaphoreType.DMA((4,)),
            pltpu.SemaphoreType.DMA((shards,)),
            pltpu.SemaphoreType.DMA((shards,)),
        ],
        compiler_params=pltpu.CompilerParams(vmem_limit_bytes=28 * 1024 * 1024),
        cost_estimate=pl.CostEstimate(
            flops=4 * pixels * channels * units,
            bytes_accessed=4 * channels * units + 4 * pixels * channels,
            transcendentals=pixels * units,
        ),
        name="mlp",
    )(
        *[s.reshape(pixels, slab) for s in slabs],
        *weights,
        gain[None],
        shift[None],
        b_in[None],
    )


def to_pair(array):
    return lax.ppermute(array, "chan", [(0, 1), (1, 0), (2, 3), (3, 2)])


def to_middle(array):
    return lax.ppermute(array, "chan", [(1, 2), (2, 1)])


def outward(array):
    return lax.ppermute(array, "chan", [(1, 0), (2, 3)])


def inward(array):
    return lax.ppermute(array, "chan", [(0, 1), (3, 2)])


def after(value, *others):
    return lax.optimization_barrier((value, *others))[0] if others else value


def add(a, b):
    return (a.astype(jnp.float32) + b.astype(jnp.float32)).astype(jnp.bfloat16)


def flipped(array, bit):
    return lax.ppermute(array, "tile", [(i, i ^ bit) for i in range(8)])


def rims(top, bottom):
    count = lax.axis_size("tile")
    forward = [(i, i + 1) for i in range(count - 1)]
    backward = [(b, a) for a, b in forward]
    return lax.ppermute(bottom, "tile", forward), lax.ppermute(top, "tile", backward)


def local(features, dw_weight, dw_bias, ln_gain, ln_bias, w_in, b_in, w_out, b_out, gamma):
    height = features.shape[0]
    rows = height // 2
    shard = w_in.shape[0]
    conv = functools.partial(conv_chunk, features=features, taps=dw_weight.T, bias=dw_bias[None])
    mlp = functools.partial(mlp_chunk, gain=ln_gain, shift=ln_bias, b_in=b_in)

    low, high = rims(features[:REACH], features[-REACH:])
    slab_0 = conv(0, rows, low=low, high=high)
    slab_1 = conv(rows, rows, low=low, high=high)

    own = jnp.concatenate([w_in, w_out.T], axis=0)
    moving = after(own, low, high)
    own_x, own_y = flipped(moving, 2), flipped(moving, 4)

    near_0, mid_in_0 = to_pair(slab_0), to_middle(slab_0)
    far_in_0, mid_out_0 = to_middle(near_0), outward(mid_in_0)
    far_out_0 = outward(far_in_0)

    begun = own_x, own_y, far_in_0, mid_out_0, slab_1
    in_xy = flipped(after(own_x, *begun)[:shard], 4)
    out_xy = flipped(after(own_y, *begun)[shard:], 2)
    near_1, mid_in_1 = to_pair(after(slab_1, *begun)), to_middle(after(slab_1, *begun))

    ready = in_xy, out_xy, far_out_0, near_1, mid_in_1
    others = flipped(after(jnp.concatenate([own, own_x, own_y], axis=0), *ready), 1)
    other_xy = flipped(after(jnp.concatenate([in_xy, out_xy], axis=0), *ready), 1)
    far_in_1, mid_out_1 = to_middle(after(near_1, *ready)), outward(after(mid_in_1, *ready))
    weights = [own, own_x, own_y, in_xy, out_xy, others, other_xy]

    line_0 = [slab_0, near_0, mid_in_0, mid_out_0, far_in_0, far_out_0]
    far_0, mid_0, pair_0, home_0 = mlp(line_0, weights)
    far_out_1 = outward(after(far_in_1, far_0))
    far_sum_0, mid_from_0 = add(far_0, inward(far_0)), inward(mid_0)

    line_1 = [slab_1, near_1, mid_in_1, mid_out_1, far_in_1, far_out_1]
    far_1, mid_1, pair_1, home_1 = mlp(line_1, weights)

    far_across_0 = to_middle(far_sum_0)
    from_pair_0 = to_pair(add(pair_0, far_across_0))

    far_sum_1, mid_from_1 = add(far_1, inward(far_1)), inward(mid_1)
    far_across_1 = to_middle(far_sum_1)
    mid_across_0 = to_middle(after(add(mid_0, mid_from_0), far_sum_1))
    mid_across_1 = to_middle(add(mid_1, mid_from_1))
    from_pair_1 = to_pair(add(pair_1, far_across_1))

    results = []
    for first, parts in (
        (0, (home_0, mid_across_0, from_pair_0)),
        (rows, (home_1, mid_across_1, from_pair_1)),
    ):
        projected = sum(part.astype(jnp.float32) for part in parts) + b_out[None, :, None]
        block = features[first : first + rows].astype(jnp.float32)
        results.append((block + gamma[None, :, None] * projected).astype(jnp.bfloat16))
    return jnp.concatenate(results, axis=0)


def plain(features, dw_weight, dw_bias, ln_gain, ln_bias, w_in, b_in, w_out, b_out, gamma):
    rows, slab, width = features.shape
    low, high = rims(features[:REACH], features[-REACH:])
    image = jnp.concatenate([low, features, high], axis=0).astype(jnp.float32)
    image = jnp.pad(image, ((0, 0), (0, 0), (REACH, REACH)))
    total = jnp.zeros((rows, slab, width), jnp.float32) + dw_bias[None, :, None]
    for a in range(SIDE):
        for b in range(SIDE):
            window = image[a : a + rows, :, b : b + width]
            total = total + window * dw_weight[:, a * SIDE + b][None, :, None]
    conv_out = lax.all_gather(total.astype(jnp.bfloat16), "chan", axis=1, tiled=True)
    values = conv_out.astype(jnp.float32)
    centered = values - jnp.mean(values, axis=1, keepdims=True)
    variance = jnp.mean(centered * centered, axis=1, keepdims=True)
    normed = centered * lax.rsqrt(variance + EPSILON) * ln_gain[None, :, None] + ln_bias[None, :, None]
    pre_act = jnp.einsum(
        "rcw,cf->rwf",
        normed.astype(jnp.bfloat16),
        lax.all_gather(w_in, "tile", axis=0, tiled=True),
        preferred_element_type=jnp.float32,
    )
    hidden = jax.nn.gelu(pre_act + b_in[None, None, :], approximate=False).astype(jnp.bfloat16)
    partial = jnp.einsum(
        "rwf,fc->rwc",
        hidden,
        lax.all_gather(w_out, "tile", axis=1, tiled=True),
        preferred_element_type=jnp.float32,
    )
    summed = lax.psum_scatter(
        partial.astype(jnp.bfloat16), "chan", scatter_dimension=2, tiled=True
    ).astype(jnp.float32)
    projected = jnp.transpose(summed + b_out[None, None, :], (0, 2, 1))
    return (features.astype(jnp.float32) + gamma[None, :, None] * projected).astype(jnp.bfloat16)


def solution(mesh):
    placed = (
        P("tile", "chan", None),
        P("chan", None),
        P("chan"),
        P(),
        P(),
        P("tile", "chan"),
        P("chan"),
        P("chan", "tile"),
        P("chan"),
        P("chan"),
    )
    cube = mesh.shape["tile"] == 8 and mesh.shape["chan"] == 4
    return jax.shard_map(
        local if cube else plain,
        mesh=mesh,
        in_specs=placed,
        out_specs=P("tile", "chan", None),
        check_vma=False,
    )
```

```python
import functools

import jax
import jax.numpy as jnp
from jax import lax
from jax.experimental import pallas as pl
from jax.experimental.pallas import tpu as pltpu
from jax.sharding import PartitionSpec as P

SIDE = 7
REACH = SIDE // 2
VMEM_LIMIT = 48 * 1024 * 1024
MLP_LIMIT = 28 * 1024 * 1024
NORM_FLOPS = 2000
EPSILON = 1e-06


def conv_kernel(plan, *refs):
    sources, taps_ref, bias_ref, out_ref, image = refs[:-4], *refs[-4:]
    rows, width, channels = out_ref.shape
    edge = (image.shape[1] - width) // 2
    blank = jnp.zeros((edge, channels), jnp.float32)
    for i, (source, row) in enumerate(plan):
        image[i, :edge, :] = blank
        image[i, edge + width :, :] = blank
        image[i, edge : edge + width, :] = sources[source][row].astype(jnp.float32).T
    bias = bias_ref[...]
    tile = 16

    def one_tile(i, carry):
        start = pl.multiple_of(i * tile, tile)
        totals = [jnp.broadcast_to(bias, (tile, channels)) for _ in range(rows)]
        for b in range(SIDE):
            for j in range(len(plan)):
                pixels = image[j, pl.ds(start + (edge - REACH + b), tile), :]
                for row in range(rows):
                    a = j - row
                    if 0 <= a < SIDE:
                        tap = SIDE * a + b
                        totals[row] = totals[row] + pixels * taps_ref[tap : tap + 1, :]
        for row in range(rows):
            out_ref[row, pl.ds(start, tile), :] = totals[row].astype(out_ref.dtype)
        return carry

    lax.fori_loop(0, width // tile, one_tile, 0)


def conv_chunk(first, rows, *, low, features, high, taps, bias):
    height, slab, width = features.shape
    names, plan = ["features"], []
    for row in range(first - REACH, first + rows + REACH):
        if row < 0:
            name, index = "low", row + REACH
        elif row < height:
            name, index = "features", row
        else:
            name, index = "high", row - height
        if name not in names:
            names.append(name)
        plan.append((names.index(name), index))
    arrays = [{"features": features, "low": low, "high": high}[name] for name in names]
    block = 128
    return pl.pallas_call(
        functools.partial(conv_kernel, tuple(plan)),
        grid=(slab // block,),
        in_specs=[pl.BlockSpec((a.shape[0], block, width), lambda i: (0, i, 0)) for a in arrays]
        + [pl.BlockSpec((t.shape[0], block), lambda i: (0, i)) for t in (taps, bias)],
        out_specs=pl.BlockSpec((rows, width, block), lambda i: (0, 0, i)),
        out_shape=jax.ShapeDtypeStruct((rows, width, slab), jnp.bfloat16),
        scratch_shapes=[pltpu.VMEM((len(plan), width + 16, block), jnp.float32)],
        compiler_params=pltpu.CompilerParams(vmem_limit_bytes=VMEM_LIMIT),
        cost_estimate=pl.CostEstimate(
            flops=2 * SIDE * SIDE * rows * slab * width,
            bytes_accessed=4 * rows * slab * width,
            transcendentals=0,
        ),
        name="depthwise",
    )(*arrays, taps, bias)


def line_places(z):
    low_half = z < 2
    return z ^ 1, jnp.where(low_half, 2, 1), jnp.where(low_half, 3, 0)


def weight_pieces(parts, shard):
    own, x, y, in_xy, out_xy, others, other_xy = parts
    three = [(own, 0), (x, 2), (y, 4)]
    ins = [(part, 0, k) for part, k in three] + [(in_xy, 0, 6), (other_xy, 0, 7)]
    outs = [(part, shard, k) for part, k in three] + [(out_xy, 0, 6), (other_xy, shard, 7)]
    for i, k in enumerate((1, 3, 5)):
        ins.append((others, 2 * shard * i, k))
        outs.append((others, 2 * shard * i + shard, k))
    return ins, outs


def start_slabs(slabs, x, sems):
    own, near, mid_inner, mid_outer, far_inner, far_outer = slabs
    slab = own.shape[1]
    z = lax.axis_index("chan")
    pair, mid, far = line_places(z)
    inner = jnp.logical_or(z == 1, z == 2)

    def slab_copy(part, place, sem):
        at = pl.ds(pl.multiple_of(place * slab, 128), slab)
        return pltpu.make_async_copy(part, x.at[:, at], sems.at[sem])

    slab_copy(own, z, 0).start()
    slab_copy(near, pair, 1).start()

    @pl.when(inner)
    def _():
        slab_copy(mid_inner, mid, 2).start()
        slab_copy(far_inner, far, 3).start()

    @pl.when(jnp.logical_not(inner))
    def _():
        slab_copy(mid_outer, mid, 2).start()
        slab_copy(far_outer, far, 3).start()

    def wait():
        slab_copy(own, z, 0).wait()
        slab_copy(near, pair, 1).wait()
        slab_copy(mid_inner, mid, 2).wait()
        slab_copy(far_inner, far, 3).wait()

    return wait


def normalize(x, out, gain_ref, shift_ref):
    pixels, channels = x.shape
    step = 256 if pixels % 256 == 0 else 64
    gain, shift = gain_ref[...], shift_ref[...]

    def block(i, carry):
        at = pl.ds(pl.multiple_of(i * step, step), step)
        values = x[at, :].astype(jnp.float32)
        average = jnp.sum(values, axis=1, keepdims=True) * (1.0 / channels)
        centered = values - average
        variance = jnp.sum(centered * centered, axis=1, keepdims=True) * (1.0 / channels)
        out[at, :] = (centered * lax.rsqrt(variance + EPSILON) * gain + shift).astype(out.dtype)
        return carry

    lax.fori_loop(0, pixels // step, block, 0)


def norm_kernel(*refs):
    gain_ref, shift_ref, out_ref, x, x_sem = refs[6:]
    start_slabs(refs[:6], x, x_sem)()
    normalize(x, out_ref, gain_ref, shift_ref)


def lift(x, w_in, b_in_ref, hidden):
    block = 256
    for f in range(0, hidden.shape[1], block):
        pre_act = jnp.dot(x[...], w_in[:, f : f + block], preferred_element_type=jnp.float32)
        pre_act = pre_act + b_in_ref[:, f : f + block]
        gelu = pre_act * (lax.erf(pre_act * (0.5**0.5)) * 0.5 + 0.5)
        hidden[:, f : f + block] = gelu.astype(hidden.dtype)


def project(hidden, w_out, out_refs):
    z = lax.axis_index("chan")
    pair, mid, far = line_places(z)
    for out_ref, place in zip(out_refs, (far, mid, pair, z), strict=True):
        rows, slab, width = out_ref.shape
        at = pl.ds(pl.multiple_of(place * slab, 16), slab)
        partial = lax.dot_general(
            w_out[at, :], hidden[...], (((1,), (1,)), ((), ())), preferred_element_type=jnp.float32
        )
        for row in range(rows):
            out_ref[row] = partial[:, row * width : (row + 1) * width].astype(out_ref.dtype)


def start_shards(pieces, target, shard, sems):
    t = lax.axis_index("tile")

    def shard_copy(piece):
        part, first, k = piece
        at = pl.ds(pl.multiple_of((t ^ k) * shard, 16), shard)
        return pltpu.make_async_copy(part.at[first : first + shard, :], target.at[at, :], sems.at[k])

    for piece in pieces:
        shard_copy(piece).start()

    def wait():
        for piece in pieces:
            shard_copy(piece).wait()

    return wait


def mlp_kernel(*refs):
    normed_ref, parts, b_in_ref, out_refs = refs[0], refs[1:8], refs[8], refs[9:13]
    w_in, w_out, hidden, in_sem, out_sem = refs[13:]
    shard = parts[0].shape[0] // 2
    ins, outs = weight_pieces(parts, shard)
    w_in_there = start_shards(ins, w_in, shard, in_sem)
    w_out_there = start_shards(outs, w_out, shard, out_sem)
    w_in_there()
    lift(normed_ref, w_in, b_in_ref, hidden)
    w_out_there()
    project(hidden, w_out, out_refs)


def norm_mlp_kernel(*refs):
    parts, (gain_ref, shift_ref, b_in_ref), out_refs = refs[6:13], refs[13:16], refs[16:20]
    x, w_in, w_out, hidden, x_sem, in_sem, out_sem = refs[20:]
    shard = parts[0].shape[0] // 2
    ins, outs = weight_pieces(parts, shard)
    x_there = start_slabs(refs[:6], x, x_sem)
    w_in_there = start_shards(ins, w_in, shard, in_sem)
    w_out_there = start_shards(outs, w_out, shard, out_sem)
    x_there()
    normalize(x, x, gain_ref, shift_ref)
    w_in_there()
    lift(x, w_in, b_in_ref, hidden)
    w_out_there()
    project(hidden, w_out, out_refs)


ANYWHERE = pl.BlockSpec(memory_space=pl.ANY)
WHOLE = pl.BlockSpec(memory_space=pltpu.VMEM)
SHARDS = 8


def norm_chunk(slabs, gain, shift):
    rows, width, slab = slabs[0].shape
    pixels, channels = rows * width, 4 * slab
    return pl.pallas_call(
        norm_kernel,
        in_specs=[ANYWHERE] * 6 + [WHOLE] * 2,
        out_specs=WHOLE,
        out_shape=jax.ShapeDtypeStruct((pixels, channels), jnp.bfloat16),
        scratch_shapes=[
            pltpu.VMEM((pixels, channels), jnp.bfloat16),
            pltpu.SemaphoreType.DMA((4,)),
        ],
        compiler_params=pltpu.CompilerParams(vmem_limit_bytes=MLP_LIMIT),
        cost_estimate=pl.CostEstimate(
            flops=NORM_FLOPS * pixels * channels, bytes_accessed=4 * pixels * channels, transcendentals=0
        ),
        name="norm",
    )(*[s.reshape(pixels, slab) for s in slabs], gain[None], shift[None])


def mlp_chunk(x, weights, rows, gain, shift, b_in):
    normed = not isinstance(x, list)
    if normed:
        pixels, channels = x.shape
        slab, width = channels // 4, pixels // rows
        inputs, vectors = [x], [b_in[None]]
        kernel, scratch = mlp_kernel, []
        specs = [WHOLE]
    else:
        _, width, slab = x[0].shape
        pixels, channels = rows * width, 4 * slab
        inputs, vectors = [s.reshape(pixels, slab) for s in x], [gain[None], shift[None], b_in[None]]
        kernel, scratch = norm_mlp_kernel, [pltpu.VMEM((pixels, channels), jnp.bfloat16)]
        specs = [ANYWHERE] * 6
    units = weights[0].shape[1]
    return pl.pallas_call(
        kernel,
        in_specs=specs + [ANYWHERE] * len(weights) + [WHOLE] * len(vectors),
        out_specs=[WHOLE] * 4,
        out_shape=[jax.ShapeDtypeStruct((rows, slab, width), jnp.bfloat16)] * 4,
        scratch_shapes=scratch
        + [
            pltpu.VMEM((channels, units), jnp.bfloat16),
            pltpu.VMEM((channels, units), jnp.bfloat16),
            pltpu.VMEM((pixels, units), jnp.bfloat16),
        ]
        + ([] if normed else [pltpu.SemaphoreType.DMA((4,))])
        + [pltpu.SemaphoreType.DMA((SHARDS,)), pltpu.SemaphoreType.DMA((SHARDS,))],
        compiler_params=pltpu.CompilerParams(vmem_limit_bytes=MLP_LIMIT),
        cost_estimate=pl.CostEstimate(
            flops=4 * pixels * channels * units,
            bytes_accessed=4 * channels * units + 4 * pixels * channels,
            transcendentals=pixels * units,
        ),
        name="mlp",
    )(*inputs, *weights, *vectors)


def to_pair(array):
    return lax.ppermute(array, "chan", [(0, 1), (1, 0), (2, 3), (3, 2)])


def to_middle(array):
    return lax.ppermute(array, "chan", [(1, 2), (2, 1)])


def outward(array):
    return lax.ppermute(array, "chan", [(1, 0), (2, 3)])


def inward(array):
    return lax.ppermute(array, "chan", [(0, 1), (3, 2)])


def after(value, *others):
    return lax.optimization_barrier((value, *others))[0] if others else value


def add(a, b):
    return (a.astype(jnp.float32) + b.astype(jnp.float32)).astype(jnp.bfloat16)


def flipped(array, bit):
    return lax.ppermute(array, "tile", [(i, i ^ bit) for i in range(8)])


def rims(top, bottom):
    count = lax.axis_size("tile")
    forward = [(i, i + 1) for i in range(count - 1)]
    backward = [(b, a) for a, b in forward]
    return lax.ppermute(bottom, "tile", forward), lax.ppermute(top, "tile", backward)


def local(features, dw_weight, dw_bias, ln_gain, ln_bias, w_in, b_in, w_out, b_out, gamma):
    height = features.shape[0]
    rows = height // 2
    shard = w_in.shape[0]
    conv = functools.partial(conv_chunk, features=features, taps=dw_weight.T, bias=dw_bias[None])
    mlp = functools.partial(mlp_chunk, rows=rows, gain=ln_gain, shift=ln_bias, b_in=b_in)

    low, high = rims(features[:REACH], features[-REACH:])
    slab_0 = conv(0, rows, low=low, high=high)
    slab_1 = conv(rows, rows, low=low, high=high)

    own = jnp.concatenate([w_in, w_out.T], axis=0)
    moving = after(own, low, high)
    own_x, own_y = flipped(moving, 2), flipped(moving, 4)

    near_0, mid_in_0 = to_pair(slab_0), to_middle(slab_0)
    far_in_0, mid_out_0 = to_middle(near_0), outward(mid_in_0)
    far_out_0 = outward(far_in_0)

    begun = own_x, own_y, far_in_0, mid_out_0, slab_1
    in_xy = flipped(after(own_x, *begun)[:shard], 4)
    out_xy = flipped(after(own_y, *begun)[shard:], 2)
    near_1, mid_in_1 = to_pair(after(slab_1, *begun)), to_middle(after(slab_1, *begun))

    ready = in_xy, out_xy, far_out_0, near_1, mid_in_1
    others = flipped(after(jnp.concatenate([own, own_x, own_y], axis=0), *ready), 1)
    other_xy = flipped(after(jnp.concatenate([in_xy, out_xy], axis=0), *ready), 1)
    far_in_1, mid_out_1 = to_middle(after(near_1, *ready)), outward(after(mid_in_1, *ready))
    weights = [own, own_x, own_y, in_xy, out_xy, others, other_xy]

    line_0 = [slab_0, near_0, mid_in_0, mid_out_0, far_in_0, far_out_0]
    normed_0 = norm_chunk(line_0, ln_gain, ln_bias)
    far_0, mid_0, pair_0, home_0 = mlp(normed_0, weights)
    far_out_1 = outward(after(far_in_1, far_0))
    far_sum_0, mid_from_0 = add(far_0, inward(far_0)), inward(mid_0)

    line_1 = [slab_1, near_1, mid_in_1, mid_out_1, far_in_1, far_out_1]
    far_1, mid_1, pair_1, home_1 = mlp(line_1, weights)

    far_across_0 = to_middle(far_sum_0)
    from_pair_0 = to_pair(add(pair_0, far_across_0))

    far_sum_1, mid_from_1 = add(far_1, inward(far_1)), inward(mid_1)
    far_across_1 = to_middle(far_sum_1)
    mid_across_0 = to_middle(after(add(mid_0, mid_from_0), far_sum_1))
    mid_across_1 = to_middle(add(mid_1, mid_from_1))
    from_pair_1 = to_pair(add(pair_1, far_across_1))

    results = []
    for first, parts in (
        (0, (home_0, mid_across_0, from_pair_0)),
        (rows, (home_1, mid_across_1, from_pair_1)),
    ):
        projected = sum(part.astype(jnp.float32) for part in parts) + b_out[None, :, None]
        block = features[first : first + rows].astype(jnp.float32)
        results.append((block + gamma[None, :, None] * projected).astype(jnp.bfloat16))
    return jnp.concatenate(results, axis=0)


def plain(features, dw_weight, dw_bias, ln_gain, ln_bias, w_in, b_in, w_out, b_out, gamma):
    rows, slab, width = features.shape
    low, high = rims(features[:REACH], features[-REACH:])
    image = jnp.concatenate([low, features, high], axis=0).astype(jnp.float32)
    image = jnp.pad(image, ((0, 0), (0, 0), (REACH, REACH)))
    total = jnp.zeros((rows, slab, width), jnp.float32) + dw_bias[None, :, None]
    for a in range(SIDE):
        for b in range(SIDE):
            window = image[a : a + rows, :, b : b + width]
            total = total + window * dw_weight[:, a * SIDE + b][None, :, None]
    conv_out = lax.all_gather(total.astype(jnp.bfloat16), "chan", axis=1, tiled=True)
    values = conv_out.astype(jnp.float32)
    centered = values - jnp.mean(values, axis=1, keepdims=True)
    variance = jnp.mean(centered * centered, axis=1, keepdims=True)
    normed = centered * lax.rsqrt(variance + EPSILON) * ln_gain[None, :, None] + ln_bias[None, :, None]
    pre_act = jnp.einsum(
        "rcw,cf->rwf",
        normed.astype(jnp.bfloat16),
        lax.all_gather(w_in, "tile", axis=0, tiled=True),
        preferred_element_type=jnp.float32,
    )
    hidden = jax.nn.gelu(pre_act + b_in[None, None, :], approximate=False).astype(jnp.bfloat16)
    partial = jnp.einsum(
        "rwf,fc->rwc",
        hidden,
        lax.all_gather(w_out, "tile", axis=1, tiled=True),
        preferred_element_type=jnp.float32,
    )
    summed = lax.psum_scatter(
        partial.astype(jnp.bfloat16), "chan", scatter_dimension=2, tiled=True
    ).astype(jnp.float32)
    projected = jnp.transpose(summed + b_out[None, None, :], (0, 2, 1))
    return (features.astype(jnp.float32) + gamma[None, :, None] * projected).astype(jnp.bfloat16)


def solution(mesh):
    placed = (
        P("tile", "chan", None),
        P("chan", None),
        P("chan"),
        P(),
        P(),
        P("tile", "chan"),
        P("chan"),
        P("chan", "tile"),
        P("chan"),
        P("chan"),
    )
    cube = mesh.shape["tile"] == 8 and mesh.shape["chan"] == 4
    return jax.shard_map(
        local if cube else plain,
        mesh=mesh,
        in_specs=placed,
        out_specs=P("tile", "chan", None),
        check_vma=False,
    )
```

```python
import functools

import jax
import jax.numpy as jnp
from jax import lax
from jax.experimental import pallas as pl
from jax.experimental.pallas import tpu as pltpu
from jax.sharding import PartitionSpec as P

SIDE = 7
REACH = SIDE // 2
VMEM_LIMIT = 48 * 1024 * 1024
MLP_LIMIT = 28 * 1024 * 1024
NORM_FLOPS = 2000
EPSILON = 1e-06


def conv_kernel(plan, *refs):
    sources, taps_ref, bias_ref, out_ref, image = refs[:-4], *refs[-4:]
    rows, width, channels = out_ref.shape
    edge = (image.shape[1] - width) // 2
    blank = jnp.zeros((edge, channels), jnp.float32)
    for i, (source, row) in enumerate(plan):
        image[i, :edge, :] = blank
        image[i, edge + width :, :] = blank
        image[i, edge : edge + width, :] = sources[source][row].astype(jnp.float32).T
    bias = bias_ref[...]
    tile = 16

    def one_tile(i, carry):
        start = pl.multiple_of(i * tile, tile)
        totals = [jnp.broadcast_to(bias, (tile, channels)) for _ in range(rows)]
        for b in range(SIDE):
            for j in range(len(plan)):
                pixels = image[j, pl.ds(start + (edge - REACH + b), tile), :]
                for row in range(rows):
                    a = j - row
                    if 0 <= a < SIDE:
                        tap = SIDE * a + b
                        totals[row] = totals[row] + pixels * taps_ref[tap : tap + 1, :]
        for row in range(rows):
            out_ref[row, pl.ds(start, tile), :] = totals[row].astype(out_ref.dtype)
        return carry

    lax.fori_loop(0, width // tile, one_tile, 0)


def conv_chunk(first, rows, *, low, features, high, taps, bias):
    height, slab, width = features.shape
    names, plan = ["features"], []
    for row in range(first - REACH, first + rows + REACH):
        if row < 0:
            name, index = "low", row + REACH
        elif row < height:
            name, index = "features", row
        else:
            name, index = "high", row - height
        if name not in names:
            names.append(name)
        plan.append((names.index(name), index))
    arrays = [{"features": features, "low": low, "high": high}[name] for name in names]
    block = 128
    return pl.pallas_call(
        functools.partial(conv_kernel, tuple(plan)),
        grid=(slab // block,),
        in_specs=[pl.BlockSpec((a.shape[0], block, width), lambda i: (0, i, 0)) for a in arrays]
        + [pl.BlockSpec((t.shape[0], block), lambda i: (0, i)) for t in (taps, bias)],
        out_specs=pl.BlockSpec((rows, width, block), lambda i: (0, 0, i)),
        out_shape=jax.ShapeDtypeStruct((rows, width, slab), jnp.bfloat16),
        scratch_shapes=[pltpu.VMEM((len(plan), width + 16, block), jnp.float32)],
        compiler_params=pltpu.CompilerParams(vmem_limit_bytes=VMEM_LIMIT),
        cost_estimate=pl.CostEstimate(
            flops=2 * SIDE * SIDE * rows * slab * width,
            bytes_accessed=4 * rows * slab * width,
            transcendentals=0,
        ),
        name="depthwise",
    )(*arrays, taps, bias)


def line_places(z):
    low_half = z < 2
    return z ^ 1, jnp.where(low_half, 2, 1), jnp.where(low_half, 3, 0)


def weight_pieces(parts, shard):
    own, x, y, in_xy, out_xy, others, other_xy = parts
    three = [(own, 0), (x, 2), (y, 4)]
    ins = [(part, 0, k) for part, k in three] + [(in_xy, 0, 6), (other_xy, 0, 7)]
    outs = [(part, shard, k) for part, k in three] + [(out_xy, 0, 6), (other_xy, shard, 7)]
    for i, k in enumerate((1, 3, 5)):
        ins.append((others, 2 * shard * i, k))
        outs.append((others, 2 * shard * i + shard, k))
    return ins, outs


def start_slabs(slabs, x, sems):
    own, near, mid_inner, mid_outer, far_inner, far_outer = slabs
    slab = own.shape[1]
    z = lax.axis_index("chan")
    pair, mid, far = line_places(z)
    inner = jnp.logical_or(z == 1, z == 2)

    def slab_copy(part, place, sem):
        at = pl.ds(pl.multiple_of(place * slab, 128), slab)
        return pltpu.make_async_copy(part, x.at[:, at], sems.at[sem])

    slab_copy(own, z, 0).start()
    slab_copy(near, pair, 1).start()

    @pl.when(inner)
    def _():
        slab_copy(mid_inner, mid, 2).start()
        slab_copy(far_inner, far, 3).start()

    @pl.when(jnp.logical_not(inner))
    def _():
        slab_copy(mid_outer, mid, 2).start()
        slab_copy(far_outer, far, 3).start()

    def wait():
        slab_copy(own, z, 0).wait()
        slab_copy(near, pair, 1).wait()
        slab_copy(mid_inner, mid, 2).wait()
        slab_copy(far_inner, far, 3).wait()

    return wait


def normalize(x, out, gain_ref, shift_ref):
    pixels, channels = x.shape
    step = 256 if pixels % 256 == 0 else 64
    gain, shift = gain_ref[...], shift_ref[...]

    def block(i, carry):
        at = pl.ds(pl.multiple_of(i * step, step), step)
        values = x[at, :].astype(jnp.float32)
        average = jnp.sum(values, axis=1, keepdims=True) * (1.0 / channels)
        centered = values - average
        variance = jnp.sum(centered * centered, axis=1, keepdims=True) * (1.0 / channels)
        out[at, :] = (centered * lax.rsqrt(variance + EPSILON) * gain + shift).astype(out.dtype)
        return carry

    lax.fori_loop(0, pixels // step, block, 0)


def norm_kernel(*refs):
    gain_ref, shift_ref, out_ref, x, x_sem = refs[6:]
    start_slabs(refs[:6], x, x_sem)()
    normalize(x, out_ref, gain_ref, shift_ref)


def lift(x, w_in, b_in_ref, hidden):
    block = 256
    for f in range(0, hidden.shape[1], block):
        pre_act = jnp.dot(x[...], w_in[:, f : f + block], preferred_element_type=jnp.float32)
        pre_act = pre_act + b_in_ref[:, f : f + block]
        gelu = pre_act * (lax.erf(pre_act * (0.5**0.5)) * 0.5 + 0.5)
        hidden[:, f : f + block] = gelu.astype(hidden.dtype)


def project(hidden, w_out, out_refs, which=slice(None)):
    z = lax.axis_index("chan")
    pair, mid, far = line_places(z)
    for out_ref, place in zip(out_refs, (far, mid, pair, z)[which], strict=True):
        rows, slab, width = out_ref.shape
        at = pl.ds(pl.multiple_of(place * slab, 16), slab)
        partial = lax.dot_general(
            w_out[at, :], hidden[...], (((1,), (1,)), ((), ())), preferred_element_type=jnp.float32
        )
        for row in range(rows):
            out_ref[row] = partial[:, row * width : (row + 1) * width].astype(out_ref.dtype)


def start_shards(pieces, target, shard, sems):
    t = lax.axis_index("tile")

    def shard_copy(piece):
        part, first, k = piece
        at = pl.ds(pl.multiple_of((t ^ k) * shard, 16), shard)
        return pltpu.make_async_copy(part.at[first : first + shard, :], target.at[at, :], sems.at[k])

    for piece in pieces:
        shard_copy(piece).start()

    def wait():
        for piece in pieces:
            shard_copy(piece).wait()

    return wait


def first_kernel(*refs):
    normed_ref, parts, b_in_ref, hidden, out_ref = refs[0], refs[1:8], refs[8], refs[9], refs[10]
    w_in, w_out, in_sem, out_sem = refs[11:]
    shard = parts[0].shape[0] // 2
    ins, outs = weight_pieces(parts, shard)
    w_in_there = start_shards(ins, w_in, shard, in_sem)
    w_out_there = start_shards(outs, w_out, shard, out_sem)
    w_in_there()
    lift(normed_ref, w_in, b_in_ref, hidden)
    w_out_there()
    project(hidden, w_out, [out_ref], slice(0, 1))


def rest_kernel(*refs):
    hidden, parts, out_refs = refs[0], refs[1:8], refs[8:11]
    w_out, out_sem = refs[11:]
    shard = parts[0].shape[0] // 2
    start_shards(weight_pieces(parts, shard)[1], w_out, shard, out_sem)()
    project(hidden, w_out, out_refs, slice(1, 4))


def split_mlp(x, weights, rows, b_in):
    pixels, channels = x.shape
    slab, width, units = channels // 4, pixels // rows, weights[0].shape[1]
    part = jax.ShapeDtypeStruct((rows, slab, width), jnp.bfloat16)
    matrix = pltpu.VMEM((channels, units), jnp.bfloat16)
    sems = pltpu.SemaphoreType.DMA((SHARDS,))
    params = pltpu.CompilerParams(vmem_limit_bytes=MLP_LIMIT)
    hidden, far = pl.pallas_call(
        first_kernel,
        in_specs=[WHOLE] + [ANYWHERE] * len(weights) + [WHOLE],
        out_specs=[WHOLE] * 2,
        out_shape=[jax.ShapeDtypeStruct((pixels, units), jnp.bfloat16), part],
        scratch_shapes=[matrix, matrix, sems, sems],
        compiler_params=params,
        cost_estimate=pl.CostEstimate(
            flops=3 * pixels * channels * units, bytes_accessed=4 * channels * units, transcendentals=0
        ),
        name="mlp_first",
    )(x, *weights, b_in[None])
    mid, pair, home = pl.pallas_call(
        rest_kernel,
        in_specs=[WHOLE] + [ANYWHERE] * len(weights),
        out_specs=[WHOLE] * 3,
        out_shape=[part] * 3,
        scratch_shapes=[matrix, sems],
        compiler_params=params,
        cost_estimate=pl.CostEstimate(
            flops=2 * pixels * channels * units, bytes_accessed=2 * channels * units, transcendentals=0
        ),
        name="mlp_rest",
    )(hidden, *weights)
    return far, mid, pair, home


def norm_mlp_kernel(*refs):
    parts, (gain_ref, shift_ref, b_in_ref), out_refs = refs[6:13], refs[13:16], refs[16:20]
    x, w_in, w_out, hidden, x_sem, in_sem, out_sem = refs[20:]
    shard = parts[0].shape[0] // 2
    ins, outs = weight_pieces(parts, shard)
    x_there = start_slabs(refs[:6], x, x_sem)
    w_in_there = start_shards(ins, w_in, shard, in_sem)
    w_out_there = start_shards(outs, w_out, shard, out_sem)
    x_there()
    normalize(x, x, gain_ref, shift_ref)
    w_in_there()
    lift(x, w_in, b_in_ref, hidden)
    w_out_there()
    project(hidden, w_out, out_refs)


ANYWHERE = pl.BlockSpec(memory_space=pl.ANY)
WHOLE = pl.BlockSpec(memory_space=pltpu.VMEM)
SHARDS = 8


def norm_chunk(slabs, gain, shift):
    rows, width, slab = slabs[0].shape
    pixels, channels = rows * width, 4 * slab
    return pl.pallas_call(
        norm_kernel,
        in_specs=[ANYWHERE] * 6 + [WHOLE] * 2,
        out_specs=WHOLE,
        out_shape=jax.ShapeDtypeStruct((pixels, channels), jnp.bfloat16),
        scratch_shapes=[
            pltpu.VMEM((pixels, channels), jnp.bfloat16),
            pltpu.SemaphoreType.DMA((4,)),
        ],
        compiler_params=pltpu.CompilerParams(vmem_limit_bytes=MLP_LIMIT),
        cost_estimate=pl.CostEstimate(
            flops=NORM_FLOPS * pixels * channels, bytes_accessed=4 * pixels * channels, transcendentals=0
        ),
        name="norm",
    )(*[s.reshape(pixels, slab) for s in slabs], gain[None], shift[None])


def mlp_chunk(slabs, weights, rows, gain, shift, b_in):
    _, width, slab = slabs[0].shape
    pixels, channels = rows * width, 4 * slab
    units = weights[0].shape[1]
    return pl.pallas_call(
        norm_mlp_kernel,
        in_specs=[ANYWHERE] * (len(slabs) + len(weights)) + [WHOLE] * 3,
        out_specs=[WHOLE] * 4,
        out_shape=[jax.ShapeDtypeStruct((rows, slab, width), jnp.bfloat16)] * 4,
        scratch_shapes=[
            pltpu.VMEM((pixels, channels), jnp.bfloat16),
            pltpu.VMEM((channels, units), jnp.bfloat16),
            pltpu.VMEM((channels, units), jnp.bfloat16),
            pltpu.VMEM((pixels, units), jnp.bfloat16),
            pltpu.SemaphoreType.DMA((4,)),
            pltpu.SemaphoreType.DMA((SHARDS,)),
            pltpu.SemaphoreType.DMA((SHARDS,)),
        ],
        compiler_params=pltpu.CompilerParams(vmem_limit_bytes=MLP_LIMIT),
        cost_estimate=pl.CostEstimate(
            flops=4 * pixels * channels * units,
            bytes_accessed=4 * channels * units + 4 * pixels * channels,
            transcendentals=pixels * units,
        ),
        name="mlp",
    )(
        *[s.reshape(pixels, slab) for s in slabs],
        *weights,
        gain[None],
        shift[None],
        b_in[None],
    )


def to_pair(array):
    return lax.ppermute(array, "chan", [(0, 1), (1, 0), (2, 3), (3, 2)])


def to_middle(array):
    return lax.ppermute(array, "chan", [(1, 2), (2, 1)])


def outward(array):
    return lax.ppermute(array, "chan", [(1, 0), (2, 3)])


def inward(array):
    return lax.ppermute(array, "chan", [(0, 1), (3, 2)])


def after(value, *others):
    return lax.optimization_barrier((value, *others))[0] if others else value


def add(a, b):
    return (a.astype(jnp.float32) + b.astype(jnp.float32)).astype(jnp.bfloat16)


def flipped(array, bit):
    return lax.ppermute(array, "tile", [(i, i ^ bit) for i in range(8)])


def rims(top, bottom):
    count = lax.axis_size("tile")
    forward = [(i, i + 1) for i in range(count - 1)]
    backward = [(b, a) for a, b in forward]
    return lax.ppermute(bottom, "tile", forward), lax.ppermute(top, "tile", backward)


def local(features, dw_weight, dw_bias, ln_gain, ln_bias, w_in, b_in, w_out, b_out, gamma):
    height = features.shape[0]
    rows = height // 2
    shard = w_in.shape[0]
    conv = functools.partial(conv_chunk, features=features, taps=dw_weight.T, bias=dw_bias[None])
    mlp = functools.partial(mlp_chunk, rows=rows, gain=ln_gain, shift=ln_bias, b_in=b_in)

    low, high = rims(features[:REACH], features[-REACH:])
    slab_0 = conv(0, rows, low=low, high=high)
    slab_1 = conv(rows, rows, low=low, high=high)

    own = jnp.concatenate([w_in, w_out.T], axis=0)
    moving = after(own, low, high)
    own_x, own_y = flipped(moving, 2), flipped(moving, 4)

    near_0, mid_in_0 = to_pair(slab_0), to_middle(slab_0)
    far_in_0, mid_out_0 = to_middle(near_0), outward(mid_in_0)
    far_out_0 = outward(far_in_0)

    begun = own_x, own_y, far_in_0, mid_out_0, slab_1
    in_xy = flipped(after(own_x, *begun)[:shard], 4)
    out_xy = flipped(after(own_y, *begun)[shard:], 2)
    near_1, mid_in_1 = to_pair(after(slab_1, *begun)), to_middle(after(slab_1, *begun))

    ready = in_xy, out_xy, far_out_0, near_1, mid_in_1
    others = flipped(after(jnp.concatenate([own, own_x, own_y], axis=0), *ready), 1)
    other_xy = flipped(after(jnp.concatenate([in_xy, out_xy], axis=0), *ready), 1)
    far_in_1, mid_out_1 = to_middle(after(near_1, *ready)), outward(after(mid_in_1, *ready))
    weights = [own, own_x, own_y, in_xy, out_xy, others, other_xy]

    line_0 = [slab_0, near_0, mid_in_0, mid_out_0, far_in_0, far_out_0]
    normed_0 = norm_chunk(line_0, ln_gain, ln_bias)
    far_0, mid_0, pair_0, home_0 = split_mlp(normed_0, weights, rows, b_in)
    far_out_1 = outward(after(far_in_1, far_0))
    far_sum_0, mid_from_0 = add(far_0, inward(far_0)), inward(mid_0)

    line_1 = [slab_1, near_1, mid_in_1, mid_out_1, far_in_1, far_out_1]
    far_1, mid_1, pair_1, home_1 = mlp(line_1, weights)

    far_across_0 = to_middle(far_sum_0)
    from_pair_0 = to_pair(add(pair_0, far_across_0))

    far_sum_1, mid_from_1 = add(far_1, inward(far_1)), inward(mid_1)
    far_across_1 = to_middle(far_sum_1)
    mid_across_0 = to_middle(after(add(mid_0, mid_from_0), far_sum_1))
    mid_across_1 = to_middle(add(mid_1, mid_from_1))
    from_pair_1 = to_pair(add(pair_1, far_across_1))

    results = []
    for first, parts in (
        (0, (home_0, mid_across_0, from_pair_0)),
        (rows, (home_1, mid_across_1, from_pair_1)),
    ):
        projected = sum(part.astype(jnp.float32) for part in parts) + b_out[None, :, None]
        block = features[first : first + rows].astype(jnp.float32)
        results.append((block + gamma[None, :, None] * projected).astype(jnp.bfloat16))
    return jnp.concatenate(results, axis=0)


def plain(features, dw_weight, dw_bias, ln_gain, ln_bias, w_in, b_in, w_out, b_out, gamma):
    rows, slab, width = features.shape
    low, high = rims(features[:REACH], features[-REACH:])
    image = jnp.concatenate([low, features, high], axis=0).astype(jnp.float32)
    image = jnp.pad(image, ((0, 0), (0, 0), (REACH, REACH)))
    total = jnp.zeros((rows, slab, width), jnp.float32) + dw_bias[None, :, None]
    for a in range(SIDE):
        for b in range(SIDE):
            window = image[a : a + rows, :, b : b + width]
            total = total + window * dw_weight[:, a * SIDE + b][None, :, None]
    conv_out = lax.all_gather(total.astype(jnp.bfloat16), "chan", axis=1, tiled=True)
    values = conv_out.astype(jnp.float32)
    centered = values - jnp.mean(values, axis=1, keepdims=True)
    variance = jnp.mean(centered * centered, axis=1, keepdims=True)
    normed = centered * lax.rsqrt(variance + EPSILON) * ln_gain[None, :, None] + ln_bias[None, :, None]
    pre_act = jnp.einsum(
        "rcw,cf->rwf",
        normed.astype(jnp.bfloat16),
        lax.all_gather(w_in, "tile", axis=0, tiled=True),
        preferred_element_type=jnp.float32,
    )
    hidden = jax.nn.gelu(pre_act + b_in[None, None, :], approximate=False).astype(jnp.bfloat16)
    partial = jnp.einsum(
        "rwf,fc->rwc",
        hidden,
        lax.all_gather(w_out, "tile", axis=1, tiled=True),
        preferred_element_type=jnp.float32,
    )
    summed = lax.psum_scatter(
        partial.astype(jnp.bfloat16), "chan", scatter_dimension=2, tiled=True
    ).astype(jnp.float32)
    projected = jnp.transpose(summed + b_out[None, None, :], (0, 2, 1))
    return (features.astype(jnp.float32) + gamma[None, :, None] * projected).astype(jnp.bfloat16)


def solution(mesh):
    placed = (
        P("tile", "chan", None),
        P("chan", None),
        P("chan"),
        P(),
        P(),
        P("tile", "chan"),
        P("chan"),
        P("chan", "tile"),
        P("chan"),
        P("chan"),
    )
    cube = mesh.shape["tile"] == 8 and mesh.shape["chan"] == 4
    return jax.shard_map(
        local if cube else plain,
        mesh=mesh,
        in_specs=placed,
        out_specs=P("tile", "chan", None),
        check_vma=False,
    )
```

```python
import functools

import jax
import jax.numpy as jnp
from jax import lax
from jax.experimental import pallas as pl
from jax.experimental.pallas import tpu as pltpu
from jax.sharding import PartitionSpec as P

SIDE = 7
REACH = SIDE // 2
VMEM_LIMIT = 48 * 1024 * 1024
MLP_LIMIT = 28 * 1024 * 1024
NORM_FLOPS = 2000
EPSILON = 1e-06


def conv_kernel(plan, *refs):
    sources, taps_ref, bias_ref, out_ref, image = refs[:-4], *refs[-4:]
    rows, width, channels = out_ref.shape
    edge = (image.shape[1] - width) // 2
    blank = jnp.zeros((edge, channels), jnp.float32)
    for i, (source, row) in enumerate(plan):
        image[i, :edge, :] = blank
        image[i, edge + width :, :] = blank
        image[i, edge : edge + width, :] = sources[source][row].astype(jnp.float32).T
    bias = bias_ref[...]
    tile = 16

    def one_tile(i, carry):
        start = pl.multiple_of(i * tile, tile)
        totals = [jnp.broadcast_to(bias, (tile, channels)) for _ in range(rows)]
        for b in range(SIDE):
            for j in range(len(plan)):
                pixels = image[j, pl.ds(start + (edge - REACH + b), tile), :]
                for row in range(rows):
                    a = j - row
                    if 0 <= a < SIDE:
                        tap = SIDE * a + b
                        totals[row] = totals[row] + pixels * taps_ref[tap : tap + 1, :]
        for row in range(rows):
            out_ref[row, pl.ds(start, tile), :] = totals[row].astype(out_ref.dtype)
        return carry

    lax.fori_loop(0, width // tile, one_tile, 0)


def conv_chunk(first, rows, *, low, features, high, taps, bias):
    height, slab, width = features.shape
    names, plan = ["features"], []
    for row in range(first - REACH, first + rows + REACH):
        if row < 0:
            name, index = "low", row + REACH
        elif row < height:
            name, index = "features", row
        else:
            name, index = "high", row - height
        if name not in names:
            names.append(name)
        plan.append((names.index(name), index))
    arrays = [{"features": features, "low": low, "high": high}[name] for name in names]
    block = 128
    return pl.pallas_call(
        functools.partial(conv_kernel, tuple(plan)),
        grid=(slab // block,),
        in_specs=[pl.BlockSpec((a.shape[0], block, width), lambda i: (0, i, 0)) for a in arrays]
        + [pl.BlockSpec((t.shape[0], block), lambda i: (0, i)) for t in (taps, bias)],
        out_specs=pl.BlockSpec((rows, width, block), lambda i: (0, 0, i)),
        out_shape=jax.ShapeDtypeStruct((rows, width, slab), jnp.bfloat16),
        scratch_shapes=[pltpu.VMEM((len(plan), width + 16, block), jnp.float32)],
        compiler_params=pltpu.CompilerParams(vmem_limit_bytes=VMEM_LIMIT),
        cost_estimate=pl.CostEstimate(
            flops=2 * SIDE * SIDE * rows * slab * width,
            bytes_accessed=4 * rows * slab * width,
            transcendentals=0,
        ),
        name="depthwise",
    )(*arrays, taps, bias)


def line_places(z):
    low_half = z < 2
    return z ^ 1, jnp.where(low_half, 2, 1), jnp.where(low_half, 3, 0)


def weight_pieces(parts, shard):
    own, x, y, in_xy, out_xy, others, other_xy = parts
    three = [(own, 0), (x, 2), (y, 4)]
    ins = [(part, 0, k) for part, k in three] + [(in_xy, 0, 6), (other_xy, 0, 7)]
    outs = [(part, shard, k) for part, k in three] + [(out_xy, 0, 6), (other_xy, shard, 7)]
    for i, k in enumerate((1, 3, 5)):
        ins.append((others, 2 * shard * i, k))
        outs.append((others, 2 * shard * i + shard, k))
    return ins, outs


def start_slabs(slabs, x, sems):
    own, near, mid_inner, mid_outer, far_inner, far_outer = slabs
    slab = own.shape[1]
    z = lax.axis_index("chan")
    pair, mid, far = line_places(z)
    inner = jnp.logical_or(z == 1, z == 2)

    def slab_copy(part, place, sem):
        at = pl.ds(pl.multiple_of(place * slab, 128), slab)
        return pltpu.make_async_copy(part, x.at[:, at], sems.at[sem])

    slab_copy(own, z, 0).start()
    slab_copy(near, pair, 1).start()

    @pl.when(inner)
    def _():
        slab_copy(mid_inner, mid, 2).start()
        slab_copy(far_inner, far, 3).start()

    @pl.when(jnp.logical_not(inner))
    def _():
        slab_copy(mid_outer, mid, 2).start()
        slab_copy(far_outer, far, 3).start()

    def wait():
        slab_copy(own, z, 0).wait()
        slab_copy(near, pair, 1).wait()
        slab_copy(mid_inner, mid, 2).wait()
        slab_copy(far_inner, far, 3).wait()

    return wait


def normalize(x, out, gain_ref, shift_ref):
    pixels, channels = x.shape
    step = 256 if pixels % 256 == 0 else 64
    gain, shift = gain_ref[...], shift_ref[...]

    def block(i, carry):
        at = pl.ds(pl.multiple_of(i * step, step), step)
        values = x[at, :].astype(jnp.float32)
        average = jnp.sum(values, axis=1, keepdims=True) * (1.0 / channels)
        centered = values - average
        variance = jnp.sum(centered * centered, axis=1, keepdims=True) * (1.0 / channels)
        out[at, :] = (centered * lax.rsqrt(variance + EPSILON) * gain + shift).astype(out.dtype)
        return carry

    lax.fori_loop(0, pixels // step, block, 0)


def norm_kernel(*refs):
    gain_ref, shift_ref, out_ref, x, x_sem = refs[6:]
    start_slabs(refs[:6], x, x_sem)()
    normalize(x, out_ref, gain_ref, shift_ref)


def lift(x, w_in, b_in_ref, hidden):
    block = 256
    for f in range(0, hidden.shape[1], block):
        pre_act = jnp.dot(x[...], w_in[:, f : f + block], preferred_element_type=jnp.float32)
        pre_act = pre_act + b_in_ref[:, f : f + block]
        gelu = pre_act * (lax.erf(pre_act * (0.5**0.5)) * 0.5 + 0.5)
        hidden[:, f : f + block] = gelu.astype(hidden.dtype)


def project(hidden, w_out, out_refs, which=slice(None)):
    z = lax.axis_index("chan")
    pair, mid, far = line_places(z)
    for out_ref, place in zip(out_refs, (far, mid, pair, z)[which], strict=True):
        rows, slab, width = out_ref.shape
        at = pl.ds(pl.multiple_of(place * slab, 16), slab)
        partial = lax.dot_general(
            w_out[at, :], hidden[...], (((1,), (1,)), ((), ())), preferred_element_type=jnp.float32
        )
        for row in range(rows):
            out_ref[row] = partial[:, row * width : (row + 1) * width].astype(out_ref.dtype)


def start_shards(pieces, target, shard, sems, wanted=None):
    t = lax.axis_index("tile")

    def shard_copy(piece):
        part, first, k = piece
        at = pl.ds(pl.multiple_of((t ^ k) * shard, 16), shard)
        return pltpu.make_async_copy(part.at[first : first + shard, :], target.at[at, :], sems.at[k])

    def on_wanted(piece, act):
        if wanted is None:
            act()
        else:
            pl.when(wanted(lax.div(t ^ piece[2], 2)))(act)

    for piece in pieces:
        on_wanted(piece, lambda piece=piece: shard_copy(piece).start())

    def wait():
        for piece in pieces:
            on_wanted(piece, lambda piece=piece: shard_copy(piece).wait())

    return wait


def first_kernel(*refs):
    normed_ref, parts, b_in_ref, hidden, out_ref = refs[0], refs[1:8], refs[8], refs[9], refs[10]
    w_in, w_out, in_sem, out_sem = refs[11:]
    shard = parts[0].shape[0] // 2
    far = line_places(lax.axis_index("chan"))[2]
    ins, outs = weight_pieces(parts, shard)
    w_in_there = start_shards(ins, w_in, shard, in_sem)
    w_out_there = start_shards(outs, w_out, shard, out_sem, lambda place: place == far)
    w_in_there()
    lift(normed_ref, w_in, b_in_ref, hidden)
    w_out_there()
    project(hidden, w_out, [out_ref], slice(0, 1))


def rest_kernel(*refs):
    hidden, parts, out_refs = refs[0], refs[1:8], refs[8:11]
    w_out, out_sem = refs[11:]
    shard = parts[0].shape[0] // 2
    far = line_places(lax.axis_index("chan"))[2]
    outs = weight_pieces(parts, shard)[1]
    start_shards(outs, w_out, shard, out_sem, lambda place: place != far)()
    project(hidden, w_out, out_refs, slice(1, 4))


def split_mlp(x, weights, rows, b_in):
    pixels, channels = x.shape
    slab, width, units = channels // 4, pixels // rows, weights[0].shape[1]
    part = jax.ShapeDtypeStruct((rows, slab, width), jnp.bfloat16)
    matrix = pltpu.VMEM((channels, units), jnp.bfloat16)
    sems = pltpu.SemaphoreType.DMA((SHARDS,))
    params = pltpu.CompilerParams(vmem_limit_bytes=MLP_LIMIT)
    hidden, far = pl.pallas_call(
        first_kernel,
        in_specs=[WHOLE] + [ANYWHERE] * len(weights) + [WHOLE],
        out_specs=[WHOLE] * 2,
        out_shape=[jax.ShapeDtypeStruct((pixels, units), jnp.bfloat16), part],
        scratch_shapes=[matrix, matrix, sems, sems],
        compiler_params=params,
        cost_estimate=pl.CostEstimate(
            flops=3 * pixels * channels * units, bytes_accessed=4 * channels * units, transcendentals=0
        ),
        name="mlp_first",
    )(x, *weights, b_in[None])
    mid, pair, home = pl.pallas_call(
        rest_kernel,
        in_specs=[WHOLE] + [ANYWHERE] * len(weights),
        out_specs=[WHOLE] * 3,
        out_shape=[part] * 3,
        scratch_shapes=[matrix, sems],
        compiler_params=params,
        cost_estimate=pl.CostEstimate(
            flops=2 * pixels * channels * units, bytes_accessed=2 * channels * units, transcendentals=0
        ),
        name="mlp_rest",
    )(hidden, *weights)
    return far, mid, pair, home


def norm_mlp_kernel(*refs):
    parts, (gain_ref, shift_ref, b_in_ref), out_refs = refs[6:13], refs[13:16], refs[16:20]
    x, w_in, w_out, hidden, x_sem, in_sem, out_sem = refs[20:]
    shard = parts[0].shape[0] // 2
    ins, outs = weight_pieces(parts, shard)
    x_there = start_slabs(refs[:6], x, x_sem)
    w_in_there = start_shards(ins, w_in, shard, in_sem)
    w_out_there = start_shards(outs, w_out, shard, out_sem)
    x_there()
    normalize(x, x, gain_ref, shift_ref)
    w_in_there()
    lift(x, w_in, b_in_ref, hidden)
    w_out_there()
    project(hidden, w_out, out_refs)


ANYWHERE = pl.BlockSpec(memory_space=pl.ANY)
WHOLE = pl.BlockSpec(memory_space=pltpu.VMEM)
SHARDS = 8


def norm_chunk(slabs, gain, shift):
    rows, width, slab = slabs[0].shape
    pixels, channels = rows * width, 4 * slab
    return pl.pallas_call(
        norm_kernel,
        in_specs=[ANYWHERE] * 6 + [WHOLE] * 2,
        out_specs=WHOLE,
        out_shape=jax.ShapeDtypeStruct((pixels, channels), jnp.bfloat16),
        scratch_shapes=[
            pltpu.VMEM((pixels, channels), jnp.bfloat16),
            pltpu.SemaphoreType.DMA((4,)),
        ],
        compiler_params=pltpu.CompilerParams(vmem_limit_bytes=MLP_LIMIT),
        cost_estimate=pl.CostEstimate(
            flops=NORM_FLOPS * pixels * channels, bytes_accessed=4 * pixels * channels, transcendentals=0
        ),
        name="norm",
    )(*[s.reshape(pixels, slab) for s in slabs], gain[None], shift[None])


def mlp_chunk(slabs, weights, rows, gain, shift, b_in):
    _, width, slab = slabs[0].shape
    pixels, channels = rows * width, 4 * slab
    units = weights[0].shape[1]
    return pl.pallas_call(
        norm_mlp_kernel,
        in_specs=[ANYWHERE] * (len(slabs) + len(weights)) + [WHOLE] * 3,
        out_specs=[WHOLE] * 4,
        out_shape=[jax.ShapeDtypeStruct((rows, slab, width), jnp.bfloat16)] * 4,
        scratch_shapes=[
            pltpu.VMEM((pixels, channels), jnp.bfloat16),
            pltpu.VMEM((channels, units), jnp.bfloat16),
            pltpu.VMEM((channels, units), jnp.bfloat16),
            pltpu.VMEM((pixels, units), jnp.bfloat16),
            pltpu.SemaphoreType.DMA((4,)),
            pltpu.SemaphoreType.DMA((SHARDS,)),
            pltpu.SemaphoreType.DMA((SHARDS,)),
        ],
        compiler_params=pltpu.CompilerParams(vmem_limit_bytes=MLP_LIMIT),
        cost_estimate=pl.CostEstimate(
            flops=4 * pixels * channels * units,
            bytes_accessed=4 * channels * units + 4 * pixels * channels,
            transcendentals=pixels * units,
        ),
        name="mlp",
    )(
        *[s.reshape(pixels, slab) for s in slabs],
        *weights,
        gain[None],
        shift[None],
        b_in[None],
    )


def to_pair(array):
    return lax.ppermute(array, "chan", [(0, 1), (1, 0), (2, 3), (3, 2)])


def to_middle(array):
    return lax.ppermute(array, "chan", [(1, 2), (2, 1)])


def outward(array):
    return lax.ppermute(array, "chan", [(1, 0), (2, 3)])


def inward(array):
    return lax.ppermute(array, "chan", [(0, 1), (3, 2)])


def after(value, *others):
    return lax.optimization_barrier((value, *others))[0] if others else value


def add(a, b):
    return (a.astype(jnp.float32) + b.astype(jnp.float32)).astype(jnp.bfloat16)


def flipped(array, bit):
    return lax.ppermute(array, "tile", [(i, i ^ bit) for i in range(8)])


def rims(top, bottom):
    count = lax.axis_size("tile")
    forward = [(i, i + 1) for i in range(count - 1)]
    backward = [(b, a) for a, b in forward]
    return lax.ppermute(bottom, "tile", forward), lax.ppermute(top, "tile", backward)


def local(features, dw_weight, dw_bias, ln_gain, ln_bias, w_in, b_in, w_out, b_out, gamma):
    height = features.shape[0]
    rows = height // 2
    shard = w_in.shape[0]
    conv = functools.partial(conv_chunk, features=features, taps=dw_weight.T, bias=dw_bias[None])
    mlp = functools.partial(mlp_chunk, rows=rows, gain=ln_gain, shift=ln_bias, b_in=b_in)

    low, high = rims(features[:REACH], features[-REACH:])
    slab_0 = conv(0, rows, low=low, high=high)
    slab_1 = conv(rows, rows, low=low, high=high)

    own = jnp.concatenate([w_in, w_out.T], axis=0)
    moving = after(own, low, high)
    own_x, own_y = flipped(moving, 2), flipped(moving, 4)

    near_0, mid_in_0 = to_pair(slab_0), to_middle(slab_0)
    far_in_0, mid_out_0 = to_middle(near_0), outward(mid_in_0)
    far_out_0 = outward(far_in_0)

    begun = own_x, own_y, far_in_0, mid_out_0, slab_1
    in_xy = flipped(after(own_x, *begun)[:shard], 4)
    out_xy = flipped(after(own_y, *begun)[shard:], 2)
    near_1, mid_in_1 = to_pair(after(slab_1, *begun)), to_middle(after(slab_1, *begun))

    ready = in_xy, out_xy, far_out_0, near_1, mid_in_1
    others = flipped(after(jnp.concatenate([own, own_x, own_y], axis=0), *ready), 1)
    other_xy = flipped(after(jnp.concatenate([in_xy, out_xy], axis=0), *ready), 1)
    far_in_1, mid_out_1 = to_middle(after(near_1, *ready)), outward(after(mid_in_1, *ready))
    weights = [own, own_x, own_y, in_xy, out_xy, others, other_xy]

    line_0 = [slab_0, near_0, mid_in_0, mid_out_0, far_in_0, far_out_0]
    normed_0 = norm_chunk(line_0, ln_gain, ln_bias)
    far_0, mid_0, pair_0, home_0 = split_mlp(normed_0, weights, rows, b_in)
    far_out_1 = outward(after(far_in_1, far_0))
    far_sum_0, mid_from_0 = add(far_0, inward(far_0)), inward(mid_0)

    line_1 = [slab_1, near_1, mid_in_1, mid_out_1, far_in_1, far_out_1]
    far_1, mid_1, pair_1, home_1 = mlp(line_1, weights)

    far_across_0 = to_middle(far_sum_0)
    from_pair_0 = to_pair(add(pair_0, far_across_0))

    far_sum_1, mid_from_1 = add(far_1, inward(far_1)), inward(mid_1)
    far_across_1 = to_middle(far_sum_1)
    mid_across_0 = to_middle(after(add(mid_0, mid_from_0), far_sum_1))
    mid_across_1 = to_middle(add(mid_1, mid_from_1))
    from_pair_1 = to_pair(add(pair_1, far_across_1))

    results = []
    for first, parts in (
        (0, (home_0, mid_across_0, from_pair_0)),
        (rows, (home_1, mid_across_1, from_pair_1)),
    ):
        projected = sum(part.astype(jnp.float32) for part in parts) + b_out[None, :, None]
        block = features[first : first + rows].astype(jnp.float32)
        results.append((block + gamma[None, :, None] * projected).astype(jnp.bfloat16))
    return jnp.concatenate(results, axis=0)


def plain(features, dw_weight, dw_bias, ln_gain, ln_bias, w_in, b_in, w_out, b_out, gamma):
    rows, slab, width = features.shape
    low, high = rims(features[:REACH], features[-REACH:])
    image = jnp.concatenate([low, features, high], axis=0).astype(jnp.float32)
    image = jnp.pad(image, ((0, 0), (0, 0), (REACH, REACH)))
    total = jnp.zeros((rows, slab, width), jnp.float32) + dw_bias[None, :, None]
    for a in range(SIDE):
        for b in range(SIDE):
            window = image[a : a + rows, :, b : b + width]
            total = total + window * dw_weight[:, a * SIDE + b][None, :, None]
    conv_out = lax.all_gather(total.astype(jnp.bfloat16), "chan", axis=1, tiled=True)
    values = conv_out.astype(jnp.float32)
    centered = values - jnp.mean(values, axis=1, keepdims=True)
    variance = jnp.mean(centered * centered, axis=1, keepdims=True)
    normed = centered * lax.rsqrt(variance + EPSILON) * ln_gain[None, :, None] + ln_bias[None, :, None]
    pre_act = jnp.einsum(
        "rcw,cf->rwf",
        normed.astype(jnp.bfloat16),
        lax.all_gather(w_in, "tile", axis=0, tiled=True),
        preferred_element_type=jnp.float32,
    )
    hidden = jax.nn.gelu(pre_act + b_in[None, None, :], approximate=False).astype(jnp.bfloat16)
    partial = jnp.einsum(
        "rwf,fc->rwc",
        hidden,
        lax.all_gather(w_out, "tile", axis=1, tiled=True),
        preferred_element_type=jnp.float32,
    )
    summed = lax.psum_scatter(
        partial.astype(jnp.bfloat16), "chan", scatter_dimension=2, tiled=True
    ).astype(jnp.float32)
    projected = jnp.transpose(summed + b_out[None, None, :], (0, 2, 1))
    return (features.astype(jnp.float32) + gamma[None, :, None] * projected).astype(jnp.bfloat16)


def solution(mesh):
    placed = (
        P("tile", "chan", None),
        P("chan", None),
        P("chan"),
        P(),
        P(),
        P("tile", "chan"),
        P("chan"),
        P("chan", "tile"),
        P("chan"),
        P("chan"),
    )
    cube = mesh.shape["tile"] == 8 and mesh.shape["chan"] == 4
    return jax.shard_map(
        local if cube else plain,
        mesh=mesh,
        in_specs=placed,
        out_specs=P("tile", "chan", None),
        check_vma=False,
    )
```
